128 devices in a mesh: ctx: 32 (over z, y, core), head: 4 (over x).
Axes of the slice: x: 4, y: 4, z: 4, core: 2. Of those that a mesh axis runs over, the one named last changes fastest.
Arguments:
- query: bfloat16 [8192, 8192], P('ctx', 'head'), may hold values from -5 to 5
- keys: bfloat16 [8192, 1024], P('ctx', 'head'), may hold values from -5 to 5
- values: bfloat16 [8192, 1024], P('ctx', 'head'), may hold values from -6 to 6
- out_saved: bfloat16 [8192, 8192], P('ctx', 'head'), may hold values from -4 to 4
- d_out: bfloat16 [8192, 8192], P('ctx', 'head'), may hold values from -6 to 6
- doc_ids: int32 [8192], P(('ctx', 'head')), may hold values from 0 to 4, as said below
- placement: int32 [32], replicated, may hold values from 0 to 31, as said below
- block_keys: int32 [32, 12], replicated, may hold values from 0 to 31, as said below
Outputs:
- grad_query: bfloat16 [8192, 8192], P('ctx', 'head')
- grad_keys: bfloat16 [8192, 1024], P('ctx', 'head')
- grad_values: bfloat16 [8192, 1024], P('ctx', 'head')
The draws below stay inside these ranges and needn't reach their ends.
Inputs may be any that keep to these rules, and one draw needn't show every extreme that they name: `placement`: A permutation of the block positions. `doc_ids`: read in packed-sequence order (block placement[s] holds stored block s), ids start at 0, never fall, and rise by one at exactly 4 positions. `block_keys`: column 0 of row b is b; every other entry of row b lies between b - 24 and b; entries may repeat.
All inputs are finite; a program needn't handle non-finite values.
Results may differ from the reference program's by a relative error of at most 0.014.
Values may be sent and summed in bfloat16 or wider, within the bound.
No kernel may reach another device: no remote copies, remote signals or barrier semaphores. Data moves between devices by JAX's collectives and lax.ppermute only.
A program may use at most 128 MiB of HBM per device.

```python
import math
import jax
import jax.numpy as jnp
from jax import lax

QH = 64
KVH = 8
HD = 128
BLOCK = 256
KSEL = 12
BLK_DEV = 1
NBLK = 32
TOKENS = 8192
N_CTX = 32


def packed_order(key):
    key_perm, key_docs = jax.random.split(key)
    order = jax.random.permutation(key_perm, NBLK).astype(jnp.int32)
    boundary_count = TOKENS // (8 * BLOCK)
    spots = jax.random.permutation(key_docs, TOKENS - 1).astype(jnp.int32) + 1
    starts = jnp.zeros((TOKENS,), jnp.int32).at[spots[:boundary_count]].set(1)
    packed_docs = jnp.cumsum(starts).astype(jnp.int32)
    stored_docs = packed_docs.reshape(NBLK, BLOCK)[order].reshape(TOKENS)
    return (order, stored_docs)


def draw_placement(key, part):
    order, stored_docs = packed_order(key)
    return order


def draw_doc_ids(key, part):
    order, stored_docs = packed_order(key)
    return stored_docs


def draw_block_keys(key, part):
    key = jax.random.fold_in(key, 7)
    blocks = jnp.arange(NBLK, dtype=jnp.int32)[:, None]
    back = jax.random.randint(key, (NBLK, KSEL), 1, 2 * KSEL + 1)
    earlier = jnp.maximum(blocks - back, 0)
    column = jnp.arange(KSEL, dtype=jnp.int32)[None, :]
    return jnp.where(column == 0, blocks, earlier).astype(jnp.int32)


def draw_query(key, part):
    key = jax.random.fold_in(key, 11)
    base = jnp.clip(jax.random.normal(key, (TOKENS, QH * HD), jnp.float32), -4.5, 4.5)
    return base.astype(jnp.bfloat16)


def draw_keys(key, part):
    key = jax.random.fold_in(key, 13)
    base = jnp.clip(jax.random.normal(key, (TOKENS, KVH * HD), jnp.float32), -4.5, 4.5)
    return base.astype(jnp.bfloat16)


def steps_of(stream_key, extent, pieces, least, high):
    level = 1.0
    for position, parts in pieces:
        steps = jax.random.uniform(jax.random.fold_in(jax.random.fold_in(stream_key, 6), position), (parts,), jnp.float32, least / len(pieces), high / len(pieces))
        level = level * jnp.repeat(jnp.exp(steps), extent[position] // parts).reshape((-1,) + (1,) * (len(extent) - 1 - position))
    return level


def bell_draw(own_key, dims, scale, reach, shards=(), kind=jnp.bfloat16):
    values = jax.random.normal(own_key, dims, jnp.float32) * scale
    if len(shards) > 0:
        values = steps_of(own_key, dims, shards, -0.22, 0.18) * values
    return jnp.clip(values, min=-reach, max=reach).astype(kind)


def setup_inputs(seed: int = 0) -> dict:
    seeds = jax.random.split(jax.random.key(seed), 9)
    return {
        "query": draw_query(jax.random.fold_in(seeds[8], 71), 0),
        "keys": draw_keys(jax.random.fold_in(seeds[8], 71), 0),
        "values": bell_draw(seeds[2], (TOKENS, KVH * HD), 1.0, 6.0, ((0, 32), (1, 4))),
        "out_saved": bell_draw(seeds[3], (TOKENS, QH * HD), 0.5, 4.0, ((0, 32), (1, 4))),
        "d_out": bell_draw(seeds[4], (TOKENS, QH * HD), 1.0, 6.0, ((0, 32), (1, 4))),
        "doc_ids": draw_doc_ids(jax.random.fold_in(seeds[8], 71), 0),
        "placement": draw_placement(jax.random.fold_in(seeds[8], 71), 0),
        "block_keys": draw_block_keys(jax.random.fold_in(seeds[8], 71), 0),
    }


def round_trip(array):
    return lax.optimization_barrier(array.astype(jnp.bfloat16)).astype(jnp.float32)

def reference(query, keys, values, out_saved, d_out, doc_ids, placement, block_keys):
    scale = 1.0 / math.sqrt(HD)
    group = QH // KVH
    slots = jnp.arange(NBLK, dtype=jnp.int32)
    inverse = lax.optimization_barrier(jnp.sum(jnp.where(placement[None, :] == slots[:, None], slots[None, :], 0), axis=1)).astype(jnp.int32)
    offsets = jnp.arange(BLOCK, dtype=jnp.int32)
    positions = (placement[:, None] * BLOCK + offsets[None, :]).reshape(TOKENS).astype(jnp.int32)

    def one_block(slot):
        begin = (slot * BLOCK).astype(jnp.int32)
        global_block = placement[slot]
        chosen = block_keys[global_block]
        same = chosen[:, None] == chosen[None, :]
        firsts = jnp.logical_not(jnp.any(jnp.tril(same, -1), axis=1))
        key_slots = inverse[chosen]
        key_rows = (key_slots[:, None] * BLOCK + offsets[None, :]).reshape(KSEL * BLOCK).astype(jnp.int32)
        query_rows = lax.dynamic_slice_in_dim(query, begin, BLOCK, 0).astype(jnp.float32).reshape(BLOCK, KVH, group, HD)
        grad_rows = lax.dynamic_slice_in_dim(d_out, begin, BLOCK, 0).astype(jnp.float32).reshape(BLOCK, KVH, group, HD)
        saved_rows = lax.dynamic_slice_in_dim(out_saved, begin, BLOCK, 0).astype(jnp.float32).reshape(BLOCK, KVH, group, HD)
        key_tile = keys[key_rows].astype(jnp.float32).reshape(KSEL * BLOCK, KVH, HD)
        value_tile = values[key_rows].astype(jnp.float32).reshape(KSEL * BLOCK, KVH, HD)
        query_docs = lax.dynamic_slice_in_dim(doc_ids, begin, BLOCK, 0)
        query_pos = lax.dynamic_slice_in_dim(positions, begin, BLOCK, 0)
        key_docs = doc_ids[key_rows]
        key_pos = positions[key_rows]
        visible = (query_docs[:, None] == key_docs[None, :]) & (key_pos[None, :] <= query_pos[:, None])
        visible = visible & jnp.repeat(firsts, BLOCK)[None, :]
        scores = jnp.einsum('ighd,jgd->ghij', query_rows, key_tile) * scale
        masked = jnp.where(visible, scores, -jnp.inf)
        row_max = lax.optimization_barrier(jnp.max(masked, axis=-1))
        row_sum = lax.optimization_barrier(jnp.sum(jnp.where(visible, jnp.exp(scores - row_max[..., None]), 0.0), axis=-1))
        log_total = row_max + jnp.log(row_sum)
        probs = round_trip(jnp.where(visible, jnp.exp(scores - log_total[..., None]), 0.0))
        delta = jnp.einsum('ighd,ighd->ghi', grad_rows, saved_rows)
        grad_probs = jnp.einsum('ighd,jgd->ghij', grad_rows, value_tile)
        grad_scores = round_trip(probs * (grad_probs - delta[..., None]))
        grad_q = jnp.einsum('ghij,jgd->ighd', grad_scores, key_tile) * scale
        grad_k = jnp.einsum('ghij,ighd->jgd', grad_scores, query_rows) * scale
        grad_v = jnp.einsum('ghij,ighd->jgd', probs, grad_rows)
        grad_q = grad_q.reshape(BLOCK, QH * HD).astype(jnp.bfloat16)
        return (grad_q, grad_k.reshape(KSEL * BLOCK, KVH * HD), grad_v.reshape(KSEL * BLOCK, KVH * HD), key_rows)

    def per_device(carry, device):
        key_total, value_total = carry
        key_part = jnp.zeros((TOKENS, KVH * HD), jnp.float32)
        value_part = jnp.zeros((TOKENS, KVH * HD), jnp.float32)
        query_list = []
        for local in range(BLK_DEV):
            grad_q, grad_k, grad_v, key_rows = one_block(device * BLK_DEV + local)
            key_part = key_part.at[key_rows].add(grad_k)
            value_part = value_part.at[key_rows].add(grad_v)
            query_list.append(grad_q)
        key_total = key_total + round_trip(key_part)
        value_total = value_total + round_trip(value_part)
        return ((key_total, value_total), jnp.stack(query_list))
    start_sums = (jnp.zeros((TOKENS, KVH * HD), jnp.float32), jnp.zeros((TOKENS, KVH * HD), jnp.float32))
    (key_total, value_total), query_blocks = lax.scan(per_device, start_sums, jnp.arange(N_CTX, dtype=jnp.int32))
    grad_query = query_blocks.reshape(TOKENS, QH * HD)
    return (grad_query, key_total.astype(jnp.bfloat16), value_total.astype(jnp.bfloat16))
```

```python
import math

import jax
import jax.numpy as jnp
from jax import lax
from jax.experimental import pallas as pl
from jax.experimental.pallas import tpu as pltpu
from jax.sharding import PartitionSpec as P

HD = 128
BLOCK = 256
GROUP = 8
WIDE = GROUP * HD
SCALE = 1.0 / math.sqrt(HD)
FACTOR = SCALE * math.log2(math.e)
HIDE = -1e30
STAT_ROWS = 16


def index_of(z, y, core):
    return ((z % 4) * 4 + y % 4) * 2 + core


def pull(array, rz, ry):
    pairs = [
        (index_of(z + rz, y + ry, core), index_of(z, y, core))
        for z in range(4)
        for y in range(4)
        for core in range(2)
    ]
    return lax.ppermute(array, "ctx", pairs)


def push(array, rz, ry):
    return pull(array, -rz, -ry)


def swap(array):
    return lax.ppermute(array, "ctx", [(i, i ^ 1) for i in range(32)])


def halves(array, core, width):
    mine = lax.dynamic_slice_in_dim(array, core * width, width, 1)
    other = lax.dynamic_slice_in_dim(array, (1 - core) * width, width, 1)
    return mine, other


def dot(a, b, contract):
    return lax.dot_general(a, b, ((contract[:1], contract[1:]), ((), ())), preferred_element_type=jnp.float32)


def fill_bias(bias, starts, table, which, key_block):
    key_pos = key_block * BLOCK + lax.broadcasted_iota(jnp.int32, (BLOCK, BLOCK), 0)
    query_pos = table[3, which] * BLOCK + lax.broadcasted_iota(jnp.int32, (1, BLOCK), 1)
    seen = (key_pos >= starts[pl.ds(which, 1), :]) & (key_pos <= query_pos)
    bias[...] = jnp.where(seen, 0.0, HIDE)


def fill_starts(starts, firsts, table, bounds):
    for which in range(2):
        begin = table[3, which] * BLOCK
        pos = begin + lax.broadcasted_iota(jnp.int32, (1, BLOCK), 1)
        row = jnp.zeros((1, BLOCK), jnp.int32)
        first = jnp.int32(0)
        for k in range(4):
            edge = bounds[0, k]
            row = jnp.maximum(row, jnp.where(pos >= edge, edge, 0))
            first = jnp.maximum(first, jnp.where(begin >= edge, edge, 0))
        starts[pl.ds(which, 1), :] = row
        firsts[which] = first


def needed(table, firsts, which, j):
    return (table[1 + which, j] > 0) & (table[0, j] * BLOCK + BLOCK - 1 >= firsts[which])


def load_blocks(first_parts, second_parts, whole, sems, base):
    copies = []
    for n in range(4):
        copies.append(
            pltpu.make_async_copy(
                first_parts[n].at[:, pl.ds(0, BLOCK), :], whole.at[:, n, 0], sems.at[base + 2 * n]
            )
        )
        copies.append(
            pltpu.make_async_copy(
                second_parts[n].at[:, pl.ds(0, BLOCK), :], whole.at[n, :, 1], sems.at[base + 2 * n + 1]
            )
        )
    return copies


def stats_kernel(table, bounds, q0, q1, d0, d1, o0, o1, *rest):
    first_keys, second_keys = rest[0:4], rest[4:8]
    lse, delta = rest[8:10]
    keys_all, bias, starts, top, total, firsts, sems = rest[10:]
    copies = load_blocks(first_keys, second_keys, keys_all, sems, 0)
    for copy in copies:
        copy.start()
    fill_starts(starts, firsts, table, bounds)
    top[...] = jnp.full(top.shape, HIDE, jnp.float32)
    total[...] = jnp.zeros(total.shape, jnp.float32)
    for which, (d_ref, o_ref) in enumerate(((d0, o0), (d1, o1))):
        for h in range(GROUP):
            cols = pl.ds(h * HD, HD)
            product = d_ref[:, cols].astype(jnp.float32) * o_ref[:, cols].astype(jnp.float32)
            delta[pl.ds(which * GROUP + h, 1), :] = jnp.sum(product.T, axis=0, keepdims=True)
    for copy in copies:
        copy.wait()

    def one_key_block(j, carry):
        rz, ry, dc = j // 8, (j // 2) % 4, j % 2
        for which, q_ref in enumerate((q0, q1)):

            @pl.when(needed(table, firsts, which, j))
            def _():
                fill_bias(bias, starts, table, which, table[0, j])
                k = keys_all[rz, ry, dc]
                for h in range(GROUP):
                    row = which * GROUP + h
                    s = dot(k, q_ref[:, pl.ds(h * HD, HD)], (1, 1)) + bias[...]
                    s = s.reshape(BLOCK // 8, 8, BLOCK)
                    old = top[row]
                    new = jnp.maximum(old, jnp.max(s, axis=0))
                    weights = jnp.exp2((s - new[None]) * FACTOR)
                    total[row] = total[row] * jnp.exp2((old - new) * FACTOR) + jnp.sum(weights, axis=0)
                    top[row] = new

        return carry

    lax.fori_loop(0, 32, one_key_block, 0)
    for row in range(2 * GROUP):
        best = jnp.max(top[row], axis=0, keepdims=True)
        amount = jnp.sum(total[row] * jnp.exp2((top[row] - best) * FACTOR), axis=0, keepdims=True)
        lse[pl.ds(row, 1), :] = best * FACTOR + jnp.log2(amount)


def grads_kernel(table, bounds, lse, delta, q0, q1, d0, d1, *rest):
    first_keys, second_keys, first_values, second_values = (rest[4 * n : 4 * n + 4] for n in range(4))
    gq = rest[16:18]
    gk = rest[18:22]
    gv = rest[22:26]
    keys_all, values_all, gk_all, gv_all, gq_all, bias, key_turned, starts, firsts, sems = rest[26:]
    copies = load_blocks(first_keys, second_keys, keys_all, sems, 0)
    copies += load_blocks(first_values, second_values, values_all, sems, 8)
    for copy in copies:
        copy.start()
    fill_starts(starts, firsts, table, bounds)
    gq_all[...] = jnp.zeros(gq_all.shape, jnp.float32)
    for copy in copies:
        copy.wait()

    def one_key_block(j, carry):
        rz, ry, dc = j // 8, (j // 2) % 4, j % 2
        any_needed = needed(table, firsts, 0, j) | needed(table, firsts, 1, j)

        @pl.when(jnp.logical_not(any_needed))
        def _():
            gk_all[rz, ry, dc] = jnp.zeros((BLOCK, HD), jnp.bfloat16)
            gv_all[ry, rz, dc] = jnp.zeros((BLOCK, HD), jnp.bfloat16)

        @pl.when(any_needed)
        def _():
            key_turned[...] = keys_all[rz, ry, dc].astype(jnp.float32).T.astype(jnp.bfloat16)

        def add_query_block(which, q_ref, d_ref, gk_sum, gv_sum):
            fill_bias(bias, starts, table, which, table[0, j])
            k = keys_all[rz, ry, dc]
            v = values_all[rz, ry, dc]
            turned = key_turned[...]
            for h in range(GROUP):
                row = which * GROUP + h
                q = q_ref[:, pl.ds(h * HD, HD)]
                d = d_ref[:, pl.ds(h * HD, HD)]
                s = dot(k, q, (1, 1))
                p = jnp.exp2(s * FACTOR + bias[...] - lse[pl.ds(row, 1), :])
                dp = dot(v, d, (1, 1))
                ds = (p * (dp - delta[pl.ds(row, 1), :])).astype(jnp.bfloat16)
                gv_sum = gv_sum + dot(p.astype(jnp.bfloat16), d, (1, 0))
                gk_sum = gk_sum + dot(ds, q, (1, 0))
                gq_all[row] += dot(turned, ds, (1, 0))
            return gk_sum, gv_sum

        zero = jnp.zeros((BLOCK, HD), jnp.float32)
        sums = (zero, zero)
        for which, (q_ref, d_ref) in enumerate(((q0, d0), (q1, d1))):
            sums = lax.cond(
                needed(table, firsts, which, j),
                lambda a, b: add_query_block(which, q_ref, d_ref, a, b),
                lambda a, b: (a, b),
                *sums,
            )

        @pl.when(any_needed)
        def _():
            gk_all[rz, ry, dc] = (sums[0] * SCALE).astype(jnp.bfloat16)
            gv_all[ry, rz, dc] = sums[1].astype(jnp.bfloat16)

        return carry

    lax.fori_loop(0, 32, one_key_block, 0)
    outs = []
    for n in range(4):
        outs.append(pltpu.make_async_copy(gk_all.at[n], gk[n], sems.at[2 * n]))
        outs.append(pltpu.make_async_copy(gv_all.at[n], gv[n], sems.at[2 * n + 1]))
    for copy in outs:
        copy.start()
    for which in range(2):
        for h in range(GROUP):
            gq[which][:, pl.ds(h * HD, HD)] = (gq_all[which * GROUP + h] * SCALE).T.astype(jnp.bfloat16)
    for copy in outs:
        copy.wait()


SMEM = pl.BlockSpec(memory_space=pltpu.SMEM)
VMEM = pl.BlockSpec(memory_space=pltpu.VMEM)
ANY = pl.BlockSpec(memory_space=pl.ANY)
BIG = pltpu.CompilerParams(vmem_limit_bytes=50 * 1024 * 1024)


def row_stats(table, bounds, queries, grads, saved, first_keys, second_keys):
    return pl.pallas_call(
        stats_kernel,
        out_shape=[jax.ShapeDtypeStruct((2 * GROUP, BLOCK), jnp.float32)] * 2,
        in_specs=[SMEM] * 2 + [VMEM] * 6 + [ANY] * 8,
        out_specs=[VMEM] * 2,
        scratch_shapes=[
            pltpu.VMEM((4, 4, 2, BLOCK, HD), jnp.bfloat16),
            pltpu.VMEM((BLOCK, BLOCK), jnp.float32),
            pltpu.VMEM((8, BLOCK), jnp.int32),
            pltpu.VMEM((2 * GROUP, 8, BLOCK), jnp.float32),
            pltpu.VMEM((2 * GROUP, 8, BLOCK), jnp.float32),
            pltpu.SMEM((2,), jnp.int32),
            pltpu.SemaphoreType.DMA((8,)),
        ],
        compiler_params=BIG,
        cost_estimate=pl.CostEstimate(flops=2_000_000_000, bytes_accessed=5 << 20, transcendentals=8 << 20),
        name="row_stats",
    )(table, bounds, *queries, *grads, *saved, *first_keys, *second_keys)


def gradients(table, bounds, lse, delta, queries, grads, first_keys, second_keys, first_values, second_values):
    part = jax.ShapeDtypeStruct((4, 2, BLOCK, HD), jnp.bfloat16)
    return pl.pallas_call(
        grads_kernel,
        out_shape=[jax.ShapeDtypeStruct((BLOCK, WIDE), jnp.bfloat16)] * 2 + [part] * 8,
        in_specs=[SMEM] * 2 + [VMEM] * 6 + [ANY] * 16,
        out_specs=[VMEM] * 2 + [ANY] * 8,
        scratch_shapes=[
            pltpu.VMEM((4, 4, 2, BLOCK, HD), jnp.bfloat16),
            pltpu.VMEM((4, 4, 2, BLOCK, HD), jnp.bfloat16),
            pltpu.VMEM((4, 4, 2, BLOCK, HD), jnp.bfloat16),
            pltpu.VMEM((4, 4, 2, BLOCK, HD), jnp.bfloat16),
            pltpu.VMEM((2 * GROUP, HD, BLOCK), jnp.float32),
            pltpu.VMEM((BLOCK, BLOCK), jnp.float32),
            pltpu.VMEM((HD, BLOCK), jnp.bfloat16),
            pltpu.VMEM((8, BLOCK), jnp.int32),
            pltpu.SMEM((2,), jnp.int32),
            pltpu.SemaphoreType.DMA((16,)),
        ],
        compiler_params=BIG,
        cost_estimate=pl.CostEstimate(flops=10_000_000_000, bytes_accessed=10 << 20, transcendentals=8 << 20),
        name="gradients",
    )(table, bounds, lse, delta, *queries, *grads, *first_keys, *second_keys, *first_values, *second_values)


def gather_first(part):
    column = jnp.stack([part] + [pull(part, r, 0) for r in (1, 2, 3)])
    return [column] + [pull(column, 0, r) for r in (1, 2, 3)]


def gather_second(part):
    column = jnp.stack([part] + [pull(part, 0, r) for r in (1, 2, 3)])
    return [column] + [pull(column, r, 0) for r in (1, 2, 3)]


def add_up(arrays):
    total = arrays[0].astype(jnp.float32)
    for array in arrays[1:]:
        total = total + array.astype(jnp.float32)
    return total


def shards(query, keys, values, out_saved, d_out, doc_ids, placement, block_keys):
    me = lax.axis_index("ctx")
    core = me % 2
    x = lax.axis_index("head")
    z, y = me // 8, (me // 2) % 4

    pos = jnp.sum(jnp.where(jnp.arange(32) == me, placement, 0)) * BLOCK + x * 64 + jnp.arange(64)
    after = jnp.where(doc_ids[None, :] <= jnp.arange(128)[:, None] % 4, pos[None, :] + 1, 0)
    edges = jnp.max(after, axis=1)[None, :]
    for_x = [lax.ppermute(edges, "head", [(i, (i + r) % 4) for i in range(4)]) for r in (1, 2, 3)]
    edges = jnp.maximum(jnp.maximum(edges, for_x[0]), jnp.maximum(for_x[1], for_x[2]))
    stat_rows = jnp.concatenate([edges // 128, edges % 128, jnp.zeros((STAT_ROWS - 2, 128), jnp.int32)], axis=0)

    k_mine, k_other = halves(keys, core, HD)
    v_mine, v_other = halves(values, core, HD)
    q_mine, q_other = halves(query, core, WIDE)
    d_mine, d_other = halves(d_out, core, WIDE)
    o_mine, o_other = halves(out_saved, core, WIDE)
    k_swap = swap(k_other)
    v_swap = swap(v_other)
    queries = (q_mine, swap(q_other))
    grads = (d_mine, swap(d_other))
    saved = (o_mine, swap(o_other))

    first_keys = gather_first(jnp.concatenate([k_mine, stat_rows.astype(jnp.bfloat16)], axis=0))
    second_keys = gather_second(k_swap)
    first_values = gather_first(v_mine)
    second_values = gather_second(v_swap)

    seen = jnp.stack([part[:, BLOCK : BLOCK + 2, :] for part in first_keys]).astype(jnp.float32)
    bounds = jnp.max(seen[:, :, 0] * 128 + seen[:, :, 1], axis=(0, 1)).astype(jnp.int32)[None, :]
    bounds = jnp.maximum(bounds, swap(bounds))

    j = jnp.arange(32)
    slots = index_of(z + j // 8, y + (j // 2) % 4, core ^ (j % 2))
    block_of = jnp.sum(jnp.where(slots[:, None] == jnp.arange(32)[None, :], placement[None, :], 0), axis=1)
    own = block_of[:2]
    chosen = jnp.sum(
        jnp.where(own[:, None, None] == jnp.arange(32)[None, :, None], block_keys[None], 0), axis=1
    )
    listed = jnp.any(chosen[:, :, None] == block_of[None, None, :], axis=1).astype(jnp.int32)
    table = jnp.concatenate([block_of[None], listed, block_of[None]], axis=0).astype(jnp.int32)

    lse, delta = row_stats(table, bounds, queries, grads, saved, first_keys, second_keys)
    outs = gradients(
        table, bounds, lse, delta, queries, grads, first_keys, second_keys, first_values, second_values
    )
    gq_mine, gq_other, gk, gv = outs[0], outs[1], outs[2:6], outs[6:10]

    gq_swap = swap(gq_other)
    gk_line = add_up([gk[0]] + [push(gk[r], r, 0) for r in (1, 2, 3)]).astype(jnp.bfloat16)
    gv_line = add_up([gv[0]] + [push(gv[r], 0, r) for r in (1, 2, 3)]).astype(jnp.bfloat16)
    gk_here = add_up([gk_line[0]] + [push(gk_line[r], 0, r) for r in (1, 2, 3)]).astype(jnp.bfloat16)
    gv_here = add_up([gv_line[0]] + [push(gv_line[r], r, 0) for r in (1, 2, 3)]).astype(jnp.bfloat16)

    def join(mine, other):
        return jnp.where(
            core == 0, jnp.concatenate([mine, other], axis=1), jnp.concatenate([other, mine], axis=1)
        )

    return (
        join(gq_mine, gq_swap),
        join(gk_here[0], swap(gk_here[1])),
        join(gv_here[0], swap(gv_here[1])),
    )


def solution(mesh):
    placed = (
        P("ctx", "head"),
        P("ctx", "head"),
        P("ctx", "head"),
        P("ctx", "head"),
        P("ctx", "head"),
        P(("ctx", "head")),
        P(),
        P(),
    )
    return jax.shard_map(
        shards,
        mesh=mesh,
        in_specs=placed,
        out_specs=(P("ctx", "head"), P("ctx", "head"), P("ctx", "head")),
        check_vma=False,
    )
```

```python
import math

import jax
import jax.numpy as jnp
from jax import lax
from jax.experimental import pallas as pl
from jax.experimental.pallas import tpu as pltpu
from jax.sharding import PartitionSpec as P

HD = 128
BLOCK = 256
GROUP = 8
WIDE = GROUP * HD
SCALE = 1.0 / math.sqrt(HD)
FACTOR = SCALE * math.log2(math.e)
HIDE = -1e30
STAT_ROWS = 16


def gray(n):
    return n ^ (n >> 1)


def index_of(corner, core):
    return (gray(corner >> 2) * 4 + gray(corner & 3)) * 2 + core


def across(array, bit):
    pairs = [(index_of(n, core), index_of(n ^ (1 << bit), core)) for n in range(16) for core in range(2)]
    return lax.ppermute(array, "ctx", pairs)


def swap(array):
    return lax.ppermute(array, "ctx", [(i, i ^ 1) for i in range(32)])


def halves(array, core, width):
    mine = lax.dynamic_slice_in_dim(array, core * width, width, 1)
    other = lax.dynamic_slice_in_dim(array, (1 - core) * width, width, 1)
    return mine, other


def dot(a, b, contract):
    return lax.dot_general(a, b, ((contract[:1], contract[1:]), ((), ())), preferred_element_type=jnp.float32)


def fill_bias(bias, starts, table, which, key_block):
    key_pos = key_block * BLOCK + lax.broadcasted_iota(jnp.int32, (BLOCK, BLOCK), 0)
    query_pos = table[3, which] * BLOCK + lax.broadcasted_iota(jnp.int32, (1, BLOCK), 1)
    seen = (key_pos >= starts[pl.ds(which, 1), :]) & (key_pos <= query_pos)
    bias[...] = jnp.where(seen, 0.0, HIDE)


def fill_starts(starts, firsts, table, bounds):
    for which in range(2):
        begin = table[3, which] * BLOCK
        pos = begin + lax.broadcasted_iota(jnp.int32, (1, BLOCK), 1)
        row = jnp.zeros((1, BLOCK), jnp.int32)
        first = jnp.int32(0)
        for k in range(4):
            edge = bounds[0, k]
            row = jnp.maximum(row, jnp.where(pos >= edge, edge, 0))
            first = jnp.maximum(first, jnp.where(begin >= edge, edge, 0))
        starts[pl.ds(which, 1), :] = row
        firsts[which] = first


def needed(table, firsts, which, j):
    return (table[1 + which, j] > 0) & (table[0, j] * BLOCK + BLOCK - 1 >= firsts[which])


def load_blocks(near, far, whole, sems, quarters):
    copies = []
    for n in quarters:
        for part, ref in enumerate((near[n], far[n])):
            copies.append(
                pltpu.make_async_copy(
                    ref.at[:, pl.ds(0, BLOCK), :], whole.at[n, pl.ds(8 * part, 8)], sems.at[2 * n + part]
                )
            )
    return copies


def stats_kernel(table, bounds, q0, q1, d0, d1, o0, o1, *rest):
    near, far = rest[0:2], rest[2:4]
    lse, delta = rest[4:6]
    keys_all, bias, starts, top, total, firsts, sems = rest[6:]
    copies = load_blocks(near, far, keys_all, sems, range(2))
    for copy in copies:
        copy.start()
    fill_starts(starts, firsts, table, bounds)
    top[...] = jnp.full(top.shape, HIDE, jnp.float32)
    total[...] = jnp.zeros(total.shape, jnp.float32)
    for which, (d_ref, o_ref) in enumerate(((d0, o0), (d1, o1))):
        for h in range(GROUP):
            cols = pl.ds(h * HD, HD)
            product = d_ref[:, cols].astype(jnp.float32) * o_ref[:, cols].astype(jnp.float32)
            delta[pl.ds(which * GROUP + h, 1), :] = jnp.sum(product.T, axis=0, keepdims=True)
    for copy in copies:
        copy.wait()

    def one_key_block(j, carry):
        rel, dc = j // 2, j % 2
        for which, q_ref in enumerate((q0, q1)):

            @pl.when(needed(table, firsts, which, j))
            def _():
                fill_bias(bias, starts, table, which, table[0, j])
                k = keys_all[dc, table[4 + dc, rel]]
                for h in range(GROUP):
                    row = which * GROUP + h
                    s = dot(k, q_ref[:, pl.ds(h * HD, HD)], (1, 1)) + bias[...]
                    s = s.reshape(BLOCK // 8, 8, BLOCK)
                    old = top[row]
                    new = jnp.maximum(old, jnp.max(s, axis=0))
                    weights = jnp.exp2((s - new[None]) * FACTOR)
                    total[row] = total[row] * jnp.exp2((old - new) * FACTOR) + jnp.sum(weights, axis=0)
                    top[row] = new

        return carry

    lax.fori_loop(0, 32, one_key_block, 0)
    for row in range(2 * GROUP):
        best = jnp.max(top[row], axis=0, keepdims=True)
        amount = jnp.sum(total[row] * jnp.exp2((top[row] - best) * FACTOR), axis=0, keepdims=True)
        lse[pl.ds(row, 1), :] = best * FACTOR + jnp.log2(amount)


def grads_kernel(table, bounds, lse, delta, q0, q1, d0, d1, *rest):
    near, far = rest[0:4], rest[4:8]
    gq = rest[8:10]
    keep, send = rest[10:14], rest[14:18]
    kv_all, grad_all, gq_all, bias, key_turned, starts, firsts, sems = rest[18:]
    copies = load_blocks(near, far, kv_all, sems, range(4))
    for copy in copies:
        copy.start()
    fill_starts(starts, firsts, table, bounds)
    gq_all[...] = jnp.zeros(gq_all.shape, jnp.float32)
    for copy in copies:
        copy.wait()

    def one_key_block(j, carry):
        rel, dc = j // 2, j % 2
        place_k, place_v = table[8 + dc, rel], table[10 + dc, rel]
        any_needed = needed(table, firsts, 0, j) | needed(table, firsts, 1, j)

        @pl.when(jnp.logical_not(any_needed))
        def _():
            grad_all[dc, place_k] = jnp.zeros((BLOCK, HD), jnp.bfloat16)
            grad_all[2 + dc, place_v] = jnp.zeros((BLOCK, HD), jnp.bfloat16)

        @pl.when(any_needed)
        def _():
            key_turned[...] = kv_all[dc, table[4 + dc, rel]].astype(jnp.float32).T.astype(jnp.bfloat16)

        def add_query_block(which, q_ref, d_ref, gk_sum, gv_sum):
            fill_bias(bias, starts, table, which, table[0, j])
            k = kv_all[dc, table[4 + dc, rel]]
            v = kv_all[2 + dc, table[6 + dc, rel]]
            turned = key_turned[...]
            for h in range(GROUP):
                row = which * GROUP + h
                q = q_ref[:, pl.ds(h * HD, HD)]
                d = d_ref[:, pl.ds(h * HD, HD)]
                s = dot(k, q, (1, 1))
                p = jnp.exp2(s * FACTOR + bias[...] - lse[pl.ds(row, 1), :])
                dp = dot(v, d, (1, 1))
                ds = (p * (dp - delta[pl.ds(row, 1), :])).astype(jnp.bfloat16)
                gv_sum = gv_sum + dot(p.astype(jnp.bfloat16), d, (1, 0))
                gk_sum = gk_sum + dot(ds, q, (1, 0))
                gq_all[row] += dot(turned, ds, (1, 0))
            return gk_sum, gv_sum

        zero = jnp.zeros((BLOCK, HD), jnp.float32)
        sums = (zero, zero)
        for which, (q_ref, d_ref) in enumerate(((q0, d0), (q1, d1))):
            sums = lax.cond(
                needed(table, firsts, which, j),
                lambda a, b: add_query_block(which, q_ref, d_ref, a, b),
                lambda a, b: (a, b),
                *sums,
            )

        @pl.when(any_needed)
        def _():
            grad_all[dc, place_k] = (sums[0] * SCALE).astype(jnp.bfloat16)
            grad_all[2 + dc, place_v] = sums[1].astype(jnp.bfloat16)

        return carry

    lax.fori_loop(0, 32, one_key_block, 0)
    outs = []
    for n in range(4):
        outs.append(pltpu.make_async_copy(grad_all.at[n, pl.ds(0, 8)], keep[n], sems.at[2 * n]))
        outs.append(pltpu.make_async_copy(grad_all.at[n, pl.ds(8, 8)], send[n], sems.at[2 * n + 1]))
    for copy in outs:
        copy.start()
    for which in range(2):
        for h in range(GROUP):
            gq[which][:, pl.ds(h * HD, HD)] = (gq_all[which * GROUP + h] * SCALE).T.astype(jnp.bfloat16)
    for copy in outs:
        copy.wait()


SMEM = pl.BlockSpec(memory_space=pltpu.SMEM)
VMEM = pl.BlockSpec(memory_space=pltpu.VMEM)
ANY = pl.BlockSpec(memory_space=pl.ANY)
BIG = pltpu.CompilerParams(vmem_limit_bytes=50 * 1024 * 1024)


def row_stats(table, bounds, queries, grads, saved, near, far):
    return pl.pallas_call(
        stats_kernel,
        out_shape=[jax.ShapeDtypeStruct((2 * GROUP, BLOCK), jnp.float32)] * 2,
        in_specs=[SMEM] * 2 + [VMEM] * 6 + [ANY] * 4,
        out_specs=[VMEM] * 2,
        scratch_shapes=[
            pltpu.VMEM((2, 16, BLOCK, HD), jnp.bfloat16),
            pltpu.VMEM((BLOCK, BLOCK), jnp.float32),
            pltpu.VMEM((8, BLOCK), jnp.int32),
            pltpu.VMEM((2 * GROUP, 8, BLOCK), jnp.float32),
            pltpu.VMEM((2 * GROUP, 8, BLOCK), jnp.float32),
            pltpu.SMEM((2,), jnp.int32),
            pltpu.SemaphoreType.DMA((8,)),
        ],
        compiler_params=BIG,
        cost_estimate=pl.CostEstimate(flops=2_000_000_000, bytes_accessed=5 << 20, transcendentals=8 << 20),
        name="row_stats",
    )(table, bounds, *queries, *grads, *saved, *near, *far)


def gradients(table, bounds, lse, delta, queries, grads, near, far):
    part = jax.ShapeDtypeStruct((8, BLOCK, HD), jnp.bfloat16)
    return pl.pallas_call(
        grads_kernel,
        out_shape=[jax.ShapeDtypeStruct((BLOCK, WIDE), jnp.bfloat16)] * 2 + [part] * 8,
        in_specs=[SMEM] * 2 + [VMEM] * 6 + [ANY] * 8,
        out_specs=[VMEM] * 2 + [ANY] * 8,
        scratch_shapes=[
            pltpu.VMEM((4, 16, BLOCK, HD), jnp.bfloat16),
            pltpu.VMEM((4, 16, BLOCK, HD), jnp.bfloat16),
            pltpu.VMEM((2 * GROUP, HD, BLOCK), jnp.float32),
            pltpu.VMEM((BLOCK, BLOCK), jnp.float32),
            pltpu.VMEM((HD, BLOCK), jnp.bfloat16),
            pltpu.VMEM((8, BLOCK), jnp.int32),
            pltpu.SMEM((2,), jnp.int32),
            pltpu.SemaphoreType.DMA((16,)),
        ],
        compiler_params=BIG,
        cost_estimate=pl.CostEstimate(flops=10_000_000_000, bytes_accessed=10 << 20, transcendentals=8 << 20),
        name="gradients",
    )(table, bounds, lse, delta, *queries, *grads, *near, *far)


def gather(parts):
    held = [part[None] for part in parts]
    for step in range(4):
        come = [across(array, (n + step) % 4) for n, array in enumerate(held)]
        if step == 3:
            return held, come
        held = [jnp.concatenate(pair, axis=0) for pair in zip(held, come)]


def reduce(keep, send):
    for step in range(4):
        come = [across(array, (n + step) % 4) for n, array in enumerate(send)]
        total = [
            (a.astype(jnp.float32) + b.astype(jnp.float32)).astype(jnp.bfloat16) for a, b in zip(keep, come)
        ]
        if step == 3:
            return total
        half = total[0].shape[0] // 2
        keep, send = [a[:half] for a in total], [a[half:] for a in total]


def shards(query, keys, values, out_saved, d_out, doc_ids, placement, block_keys):
    me = lax.axis_index("ctx")
    core = me % 2
    x = lax.axis_index("head")
    z, y = me // 8, (me // 2) % 4

    k_mine, k_other = halves(keys, core, HD)
    v_mine, v_other = halves(values, core, HD)
    k_swap = swap(k_other)
    v_swap = swap(v_other)

    pos = jnp.sum(jnp.where(jnp.arange(32) == me, placement, 0)) * BLOCK + x * 64 + jnp.arange(64)
    after = jnp.where(doc_ids[None, :] <= jnp.arange(128)[:, None] % 4, pos[None, :] + 1, 0)
    edges = jnp.max(after, axis=1)[None, :]
    for_x = [lax.ppermute(edges, "head", [(i, (i + r) % 4) for i in range(4)]) for r in (1, 2, 3)]
    edges = jnp.maximum(jnp.maximum(edges, for_x[0]), jnp.maximum(for_x[1], for_x[2]))
    stat_rows = jnp.concatenate([edges // 128, edges % 128, jnp.zeros((STAT_ROWS - 2, 128), jnp.int32)], axis=0)

    first = jnp.concatenate([k_mine, stat_rows.astype(jnp.bfloat16)], axis=0)
    near, far = gather([first, k_swap, v_mine, v_swap])

    query, d_out, out_saved, _ = lax.optimization_barrier((query, d_out, out_saved, v_swap))
    q_mine, q_other = halves(query, core, WIDE)
    d_mine, d_other = halves(d_out, core, WIDE)
    o_mine, o_other = halves(out_saved, core, WIDE)
    queries = (q_mine, swap(q_other))
    grads = (d_mine, swap(d_other))
    saved = (o_mine, swap(o_other))

    seen = jnp.concatenate([part[:, BLOCK : BLOCK + 2, :] for part in (near[0], far[0])]).astype(jnp.float32)
    bounds = jnp.max(seen[:, 0] * 128 + seen[:, 1], axis=0).astype(jnp.int32)[None, :]
    bounds = jnp.maximum(bounds, swap(bounds))

    j = jnp.arange(32)
    slots = index_of((gray(z) * 4 + gray(y)) ^ (j // 2), core ^ (j % 2))
    block_of = jnp.sum(jnp.where(slots[:, None] == jnp.arange(32)[None, :], placement[None, :], 0), axis=1)
    own = block_of[:2]
    chosen = jnp.sum(jnp.where(own[:, None, None] == jnp.arange(32)[None, :, None], block_keys[None], 0), axis=1)
    listed = jnp.any(chosen[:, :, None] == block_of[None, None, :], axis=1).astype(jnp.int32)
    bits = [[(rel >> bit) & 1 for bit in range(4)] for rel in range(32)]
    gathered = [[sum(b[(n + k) % 4] << k for k in range(4)) for b in bits] for n in range(4)]
    reduced = [[sum(b[(n + k) % 4] << (3 - k) for k in range(4)) for b in bits] for n in range(4)]
    table = jnp.concatenate(
        [block_of[None], listed, block_of[None], jnp.array(gathered), jnp.array(reduced)], axis=0
    ).astype(jnp.int32)

    lse, delta = row_stats(table, bounds, queries, grads, saved, near[:2], far[:2])
    outs = gradients(table, bounds, lse, delta, queries, grads, near, far)
    gq_mine, gq_other, keep, send = outs[0], outs[1], outs[2:6], outs[6:10]

    gk_mine, gk_other, gv_mine, gv_other = reduce(keep, send)
    gq_swap = swap(gq_other)

    def join(mine, other):
        return jnp.where(
            core == 0, jnp.concatenate([mine, other], axis=1), jnp.concatenate([other, mine], axis=1)
        )

    return (
        join(gq_mine, gq_swap),
        join(gk_mine[0], swap(gk_other[0])),
        join(gv_mine[0], swap(gv_other[0])),
    )


def solution(mesh):
    placed = (
        P("ctx", "head"),
        P("ctx", "head"),
        P("ctx", "head"),
        P("ctx", "head"),
        P("ctx", "head"),
        P(("ctx", "head")),
        P(),
        P(),
    )
    return jax.shard_map(
        shards,
        mesh=mesh,
        in_specs=placed,
        out_specs=(P("ctx", "head"), P("ctx", "head"), P("ctx", "head")),
        check_vma=False,
    )
```

```python
import math

import jax
import jax.numpy as jnp
from jax import lax
from jax.experimental import pallas as pl
from jax.experimental.pallas import tpu as pltpu
from jax.sharding import PartitionSpec as P

HD = 128
BLOCK = 256
GROUP = 8
WIDE = GROUP * HD
SCALE = 1.0 / math.sqrt(HD)
FACTOR = SCALE * math.log2(math.e)
HIDE = -1e30
STAT_ROWS = 16


def gray(n):
    return n ^ (n >> 1)


def index_of(corner, core):
    return (gray(corner >> 2) * 4 + gray(corner & 3)) * 2 + core


def across(array, bit):
    pairs = [(index_of(n, core), index_of(n ^ (1 << bit), core)) for n in range(16) for core in range(2)]
    return lax.ppermute(array, "ctx", pairs)


def swap(array):
    return lax.ppermute(array, "ctx", [(i, i ^ 1) for i in range(32)])


def halves(array, core, width):
    mine = lax.dynamic_slice_in_dim(array, core * width, width, 1)
    other = lax.dynamic_slice_in_dim(array, (1 - core) * width, width, 1)
    return mine, other


def dot(a, b, contract):
    return lax.dot_general(a, b, ((contract[:1], contract[1:]), ((), ())), preferred_element_type=jnp.float32)


def fold(op, array):
    while array.shape[0] > 1:
        half = array.shape[0] // 2
        array = op(array[:half], array[half:])
    return array[0]


def fill_bias(bias, starts, table, which, key_block):
    key_pos = key_block * BLOCK + lax.broadcasted_iota(jnp.int32, (BLOCK, BLOCK), 0)
    query_pos = table[3, which] * BLOCK + lax.broadcasted_iota(jnp.int32, (1, BLOCK), 1)
    seen = (key_pos >= starts[pl.ds(which, 1), :]) & (key_pos <= query_pos)
    bias[...] = jnp.where(seen, 0.0, HIDE)


def fill_starts(starts, firsts, table, bounds):
    for which in range(2):
        begin = table[3, which] * BLOCK
        pos = begin + lax.broadcasted_iota(jnp.int32, (1, BLOCK), 1)
        row = jnp.zeros((1, BLOCK), jnp.int32)
        first = jnp.int32(0)
        for k in range(4):
            edge = bounds[0, k]
            row = jnp.maximum(row, jnp.where(pos >= edge, edge, 0))
            first = jnp.maximum(first, jnp.where(begin >= edge, edge, 0))
        starts[pl.ds(which, 1), :] = row
        firsts[which] = first


def needed(table, firsts, which, j):
    return (table[1 + which, j] > 0) & (table[0, j] * BLOCK + BLOCK - 1 >= firsts[which])


def load_blocks(near, far, whole, sems, quarters):
    copies = []
    for n in quarters:
        for part, ref in enumerate((near[n], far[n])):
            copies.append(
                pltpu.make_async_copy(
                    ref.at[:, pl.ds(0, BLOCK), :], whole.at[n, pl.ds(8 * part, 8)], sems.at[2 * n + part]
                )
            )
    return copies


def prepare_kernel(core, query, d_out, saved, swapped, q_turned, d_turned, delta, own, sems):
    begin = pl.multiple_of(core[0] * WIDE, WIDE)
    copies = [
        pltpu.make_async_copy(ref.at[:, pl.ds(begin, WIDE)], own.at[n], sems.at[n])
        for n, ref in enumerate((query, d_out, saved))
    ]
    for copy in copies:
        copy.start()
    for which, source in ((1, swapped), (0, own)):
        if which == 0:
            for copy in copies:
                copy.wait()
        for h in range(GROUP):
            row = which * GROUP + h
            cols = pl.ds(h * HD, HD)
            q_turned[row] = source[0, :, cols].T
            turned = source[1, :, cols].T
            d_turned[row] = turned
            product = turned.astype(jnp.float32) * source[2, :, cols].T.astype(jnp.float32)
            delta[pl.ds(row, 1), :] = jnp.sum(product, axis=0, keepdims=True)


def main_kernel(table, bounds, q_turned, d_turned, delta, *rest):
    near, far = rest[0:4], rest[4:8]
    gq = rest[8:10]
    keep, send = rest[10:14], rest[14:18]
    kv_all, grad_all, gq_all, top, total, lse, bias, key_turned, starts, firsts, sems = rest[18:]
    copies = load_blocks(near, far, kv_all, sems, range(4))
    for copy in copies:
        copy.start()
    fill_starts(starts, firsts, table, bounds)
    top[...] = jnp.full(top.shape, HIDE, jnp.float32)
    total[...] = jnp.zeros(total.shape, jnp.float32)
    for copy in copies[:4]:
        copy.wait()

    def add_to_sums(j, carry):
        rel, dc = j // 2, j % 2
        for which in range(2):

            @pl.when(needed(table, firsts, which, j))
            def _():
                fill_bias(bias, starts, table, which, table[0, j])
                k = kv_all[dc, table[4 + dc, rel]]

                def update(h, s):
                    row = which * GROUP + h
                    old, amount = top[row], total[row]
                    for c in range(0, BLOCK, 64):
                        part = (s[c : c + 64] * FACTOR + bias[c : c + 64, :]).reshape(8, 8, BLOCK)
                        new = jnp.maximum(old, fold(jnp.maximum, part))
                        weights = jnp.exp2(part - new[None])
                        amount = amount * jnp.exp2(old - new) + fold(jnp.add, weights)
                        old = new
                    total[row] = amount
                    top[row] = old

                early = {}
                for step in range(GROUP + 1):
                    if step < GROUP:
                        early[step] = dot(k, q_turned[which * GROUP + step], (1, 0))
                    if step >= 1:
                        update(step - 1, early.pop(step - 1))

        return carry

    lax.fori_loop(0, 32, add_to_sums, 0)
    for row in range(2 * GROUP):
        best = jnp.max(top[row], axis=0, keepdims=True)
        amount = jnp.sum(total[row] * jnp.exp2(top[row] - best), axis=0, keepdims=True)
        lse[pl.ds(row, 1), :] = best + jnp.log2(amount)
    gq_all[...] = jnp.zeros(gq_all.shape, jnp.float32)
    for copy in copies[4:]:
        copy.wait()

    def add_gradients(j, carry):
        rel, dc = j // 2, j % 2
        place_k, place_v = table[8 + dc, rel], table[10 + dc, rel]
        any_needed = needed(table, firsts, 0, j) | needed(table, firsts, 1, j)

        @pl.when(jnp.logical_not(any_needed))
        def _():
            grad_all[dc, place_k] = jnp.zeros((BLOCK, HD), jnp.bfloat16)
            grad_all[2 + dc, place_v] = jnp.zeros((BLOCK, HD), jnp.bfloat16)

        @pl.when(any_needed)
        def _():
            key_turned[...] = kv_all[dc, table[4 + dc, rel]].T

        def add_query_block(which, gk_sum, gv_sum):
            fill_bias(bias, starts, table, which, table[0, j])
            k = kv_all[dc, table[4 + dc, rel]]
            v = kv_all[2 + dc, table[6 + dc, rel]]
            turned = key_turned[...]

            def first(h):
                row = which * GROUP + h
                return dot(k, q_turned[row], (1, 0)), dot(v, d_turned[row], (1, 0))

            def middle(h, s, dp):
                row = which * GROUP + h
                p = jnp.exp2(s * FACTOR + bias[...] - lse[pl.ds(row, 1), :])
                ds = (p * (dp - delta[pl.ds(row, 1), :])).astype(jnp.bfloat16)
                return p.astype(jnp.bfloat16), ds

            early, late = {}, {}
            for step in range(GROUP + 2):
                if step < GROUP:
                    early[step] = first(step)
                h = step - 1
                if 0 <= h < GROUP:
                    late[h] = middle(h, *early.pop(h))
                h = step - 2
                if 0 <= h < GROUP:
                    row = which * GROUP + h
                    p, ds = late.pop(h)
                    gv_sum = gv_sum + dot(d_turned[row], p, (1, 1))
                    gk_sum = gk_sum + dot(q_turned[row], ds, (1, 1))
                    gq_all[row] += dot(turned, ds, (1, 0))
            return gk_sum, gv_sum

        zero = jnp.zeros((HD, BLOCK), jnp.float32)
        sums = (zero, zero)
        for which in range(2):
            sums = lax.cond(
                needed(table, firsts, which, j),
                lambda a, b: add_query_block(which, a, b),
                lambda a, b: (a, b),
                *sums,
            )

        @pl.when(any_needed)
        def _():
            grad_all[dc, place_k] = (sums[0] * SCALE).T.astype(jnp.bfloat16)
            grad_all[2 + dc, place_v] = sums[1].T.astype(jnp.bfloat16)

        return carry

    lax.fori_loop(0, 32, add_gradients, 0)
    outs = []
    for n in range(4):
        outs.append(pltpu.make_async_copy(grad_all.at[n, pl.ds(8, 8)], send[n], sems.at[2 * n + 1]))
        outs.append(pltpu.make_async_copy(grad_all.at[n, pl.ds(0, 8)], keep[n], sems.at[2 * n]))
    for copy in outs:
        copy.start()
    for which in range(2):
        for h in range(GROUP):
            gq[which][:, pl.ds(h * HD, HD)] = (gq_all[which * GROUP + h] * SCALE).T.astype(jnp.bfloat16)
    for copy in outs:
        copy.wait()


SMEM = pl.BlockSpec(memory_space=pltpu.SMEM)
VMEM = pl.BlockSpec(memory_space=pltpu.VMEM)
ANY = pl.BlockSpec(memory_space=pl.ANY)
TURNED = jax.ShapeDtypeStruct((2 * GROUP, HD, BLOCK), jnp.bfloat16)


def prepare(core, query, d_out, saved, swapped):
    return pl.pallas_call(
        prepare_kernel,
        out_shape=[TURNED, TURNED, jax.ShapeDtypeStruct((2 * GROUP, BLOCK), jnp.float32)],
        in_specs=[SMEM] + [ANY] * 3 + [VMEM],
        out_specs=[VMEM] * 3,
        scratch_shapes=[pltpu.VMEM((3, BLOCK, WIDE), jnp.bfloat16), pltpu.SemaphoreType.DMA((3,))],
        compiler_params=pltpu.CompilerParams(vmem_limit_bytes=20 * 1024 * 1024),
        cost_estimate=pl.CostEstimate(flops=2_000_000, bytes_accessed=5 << 20, transcendentals=0),
        name="prepare",
    )(core, query, d_out, saved, swapped)


def gradients(table, bounds, q_turned, d_turned, delta, near, far):
    part = jax.ShapeDtypeStruct((8, BLOCK, HD), jnp.bfloat16)
    return pl.pallas_call(
        main_kernel,
        out_shape=[jax.ShapeDtypeStruct((BLOCK, WIDE), jnp.bfloat16)] * 2 + [part] * 8,
        in_specs=[SMEM] * 2 + [VMEM] * 3 + [ANY] * 8,
        out_specs=[VMEM] * 2 + [ANY] * 8,
        scratch_shapes=[
            pltpu.VMEM((4, 16, BLOCK, HD), jnp.bfloat16),
            pltpu.VMEM((4, 16, BLOCK, HD), jnp.bfloat16),
            pltpu.VMEM((2 * GROUP, HD, BLOCK), jnp.float32),
            pltpu.VMEM((2 * GROUP, 8, BLOCK), jnp.float32),
            pltpu.VMEM((2 * GROUP, 8, BLOCK), jnp.float32),
            pltpu.VMEM((2 * GROUP, BLOCK), jnp.float32),
            pltpu.VMEM((BLOCK, BLOCK), jnp.float32),
            pltpu.VMEM((HD, BLOCK), jnp.bfloat16),
            pltpu.VMEM((8, BLOCK), jnp.int32),
            pltpu.SMEM((2,), jnp.int32),
            pltpu.SemaphoreType.DMA((8,)),
        ],
        compiler_params=pltpu.CompilerParams(vmem_limit_bytes=40 * 1024 * 1024),
        cost_estimate=pl.CostEstimate(flops=12_000_000_000, bytes_accessed=10 << 20, transcendentals=16 << 20),
        name="gradients",
    )(table, bounds, q_turned, d_turned, delta, *near, *far)


def gather(parts, edges, late):
    held = [part[None] for part in parts]
    for step in range(4):
        sent = list(held)
        rows = jnp.broadcast_to(pack_edges(edges)[None], (held[0].shape[0], STAT_ROWS, HD))
        sent[0] = jnp.concatenate([held[0], rows], axis=1)
        come = [across(sent[n], (n + step) % 4) for n in (1, 2, 3, 0)]
        come = come[3:] + come[:3]
        edges = jnp.maximum(edges, unpack_edges(come[0]))
        if step == 3:
            return held, come, edges, late
        come[0] = come[0][:, :BLOCK]
        held = [jnp.concatenate(pair, axis=0) for pair in zip(held, come)]
        if step == 2:
            held, late = lax.optimization_barrier((held, late))
        else:
            held = lax.optimization_barrier(held)


def pack_edges(edges):
    spare = jnp.zeros((STAT_ROWS - 2, HD), jnp.int32)
    return jnp.concatenate([edges // 128, edges % 128, spare], axis=0).astype(jnp.bfloat16)


def unpack_edges(array):
    rows = array[:1, BLOCK : BLOCK + 2].astype(jnp.float32)
    return (rows[:, 0] * 128 + rows[:, 1]).astype(jnp.int32)


def reduce(keep, send):
    for step in range(4):
        come = [across(array, (n + step) % 4) for n, array in enumerate(send)]
        total = [
            (a.astype(jnp.float32) + b.astype(jnp.float32)).astype(jnp.bfloat16) for a, b in zip(keep, come)
        ]
        if step == 3:
            return total
        half = total[0].shape[0] // 2
        keep, send = [a[:half] for a in total], [a[half:] for a in total]


def shards(query, keys, values, out_saved, d_out, doc_ids, placement, block_keys):
    me = lax.axis_index("ctx")
    core = me % 2
    x = lax.axis_index("head")
    z, y = me // 8, (me // 2) % 4

    pos = jnp.sum(jnp.where(jnp.arange(32) == me, placement, 0)) * BLOCK + x * 64 + jnp.arange(64)
    after = jnp.where(doc_ids[None, :] <= jnp.arange(128)[:, None] % 4, pos[None, :] + 1, 0)
    edges = jnp.max(after, axis=1)[None, :]
    for_x = [lax.ppermute(edges, "head", [(i, (i + r) % 4) for i in range(4)]) for r in (1, 2, 3)]
    edges = jnp.maximum(jnp.maximum(edges, for_x[0]), jnp.maximum(for_x[1], for_x[2]))
    edges = jnp.maximum(edges, swap(edges))

    k_mine, k_other = halves(keys, core, HD)
    v_mine, v_other = halves(values, core, HD)
    kv_swap = swap(jnp.stack([k_other, v_other]))
    near, far, bounds, late = gather(
        [k_mine, kv_swap[0], v_mine, kv_swap[1]], edges, (query, d_out, out_saved)
    )

    query, d_out, out_saved = late
    others = jnp.stack([lax.dynamic_slice_in_dim(a, (1 - core) * WIDE, WIDE, 1) for a in late])
    turned = prepare(core.reshape(1).astype(jnp.int32), query, d_out, out_saved, swap(others))

    j = jnp.arange(32)
    slots = index_of((gray(z) * 4 + gray(y)) ^ (j // 2), core ^ (j % 2))
    block_of = jnp.sum(jnp.where(slots[:, None] == jnp.arange(32)[None, :], placement[None, :], 0), axis=1)
    own = block_of[:2]
    chosen = jnp.sum(jnp.where(own[:, None, None] == jnp.arange(32)[None, :, None], block_keys[None], 0), axis=1)
    listed = jnp.any(chosen[:, :, None] == block_of[None, None, :], axis=1).astype(jnp.int32)
    bits = [[(rel >> bit) & 1 for bit in range(4)] for rel in range(32)]
    gathered = [[sum(b[(n + k) % 4] << k for k in range(4)) for b in bits] for n in range(4)]
    reduced = [[sum(b[(n + k) % 4] << (3 - k) for k in range(4)) for b in bits] for n in range(4)]
    table = jnp.concatenate(
        [block_of[None], listed, block_of[None], jnp.array(gathered), jnp.array(reduced)], axis=0
    ).astype(jnp.int32)

    outs = gradients(table, bounds, *turned, near, far)
    gq_mine, gq_other, keep, send = outs[0], outs[1], outs[2:6], outs[6:10]

    gk_mine, gk_other, gv_mine, gv_other = reduce(keep, send)
    gq_swap = swap(gq_other)

    def join(mine, other):
        return jnp.where(
            core == 0, jnp.concatenate([mine, other], axis=1), jnp.concatenate([other, mine], axis=1)
        )

    return (
        join(gq_mine, gq_swap),
        join(gk_mine[0], swap(gk_other[0])),
        join(gv_mine[0], swap(gv_other[0])),
    )


def solution(mesh):
    placed = (
        P("ctx", "head"),
        P("ctx", "head"),
        P("ctx", "head"),
        P("ctx", "head"),
        P("ctx", "head"),
        P(("ctx", "head")),
        P(),
        P(),
    )
    return jax.shard_map(
        shards,
        mesh=mesh,
        in_specs=placed,
        out_specs=(P("ctx", "head"), P("ctx", "head"), P("ctx", "head")),
        check_vma=False,
    )
```

```python
import math

import jax
import jax.numpy as jnp
from jax import lax
from jax.experimental import pallas as pl
from jax.experimental.pallas import tpu as pltpu
from jax.sharding import PartitionSpec as P

HD = 128
BLOCK = 256
GROUP = 8
WIDE = GROUP * HD
SCALE = 1.0 / math.sqrt(HD)
FACTOR = SCALE * math.log2(math.e)
HIDE = -1e30
STAT_ROWS = 16


def gray(n):
    return n ^ (n >> 1)


def index_of(corner, core):
    return (gray(corner >> 2) * 4 + gray(corner & 3)) * 2 + core


def across(array, bit, turn=0):
    pairs = [(index_of(n, core), index_of(n ^ (1 << bit), core ^ turn)) for n in range(16) for core in range(2)]
    return lax.ppermute(array, "ctx", pairs)


def swap(array):
    return lax.ppermute(array, "ctx", [(i, i ^ 1) for i in range(32)])


def dot(a, b, contract):
    return lax.dot_general(a, b, ((contract[:1], contract[1:]), ((), ())), preferred_element_type=jnp.float32)


def fold(op, array):
    while array.shape[0] > 1:
        half = array.shape[0] // 2
        array = op(array[:half], array[half:])
    return array[0]


def fill_bias(bias, starts, table, which, key_block):
    key_pos = key_block * BLOCK + lax.broadcasted_iota(jnp.int32, (BLOCK, BLOCK), 0)
    query_pos = table[3, which] * BLOCK + lax.broadcasted_iota(jnp.int32, (1, BLOCK), 1)
    seen = (key_pos >= starts[pl.ds(which, 1), :]) & (key_pos <= query_pos)
    bias[...] = jnp.where(seen, 0.0, HIDE)


def fill_starts(starts, firsts, table, bounds):
    for which in range(2):
        begin = table[3, which] * BLOCK
        pos = begin + lax.broadcasted_iota(jnp.int32, (1, BLOCK), 1)
        row = jnp.zeros((1, BLOCK), jnp.int32)
        first = jnp.int32(0)
        for k in range(4):
            edge = bounds[0, k]
            row = jnp.maximum(row, jnp.where(pos >= edge, edge, 0))
            first = jnp.maximum(first, jnp.where(begin >= edge, edge, 0))
        starts[pl.ds(which, 1), :] = row
        firsts[which] = first


def needed(table, firsts, which, j):
    return (table[1 + which, j] > 0) & (table[0, j] * BLOCK + BLOCK - 1 >= firsts[which])


def load_blocks(near, far, whole, sems, quarters):
    copies = []
    for n in quarters:
        for part, ref in enumerate((near[n], far[n])):
            copies.append(
                pltpu.make_async_copy(
                    ref.at[:, pl.ds(0, BLOCK), :], whole.at[n, pl.ds(8 * part, 8)], sems.at[2 * n + part]
                )
            )
    return copies


def pack_keys_kernel(placement, doc_ids, keys, values, k_mine, v_mine, k_other, v_other, edges, sems):
    me = lax.axis_index("ctx")
    core = lax.rem(me, 2)
    copies = []
    for n, (ref, mine, other) in enumerate(((keys, k_mine, k_other), (values, v_mine, v_other))):
        for part, (out, head) in enumerate(((other, 1 - core), (mine, core))):
            cols = pl.ds(pl.multiple_of(head * HD, HD), HD)
            copies.append(pltpu.make_async_copy(ref.at[:, cols], out, sems.at[2 * n + part]))
    for copy in copies:
        copy.start()
    begin = placement[me] * BLOCK + lax.axis_index("head") * 64
    lane = lax.broadcasted_iota(jnp.int32, (1, HD), 1)
    row = jnp.zeros((1, HD), jnp.int32)
    for k in range(4):
        count = jnp.sum((doc_ids[...] <= k).astype(jnp.int32), axis=1, keepdims=True)
        row = jnp.where(lane == k, jnp.where(count > 0, begin + count, 0), row)
    edges[...] = row
    for copy in copies:
        copy.wait()


def pack_queries_kernel(query, d_out, saved, other, sems):
    core = lax.rem(lax.axis_index("ctx"), 2)
    cols = pl.ds(pl.multiple_of((1 - core) * WIDE, WIDE), WIDE)
    copies = [
        pltpu.make_async_copy(ref.at[:, cols], other.at[n], sems.at[n])
        for n, ref in enumerate((query, d_out, saved))
    ]
    for copy in copies:
        copy.start()
    for copy in copies:
        copy.wait()


def prepare_kernel(query, d_out, saved, swapped, after, q_turned, d_turned, delta, own, sems):
    del after
    begin = pl.multiple_of(lax.rem(lax.axis_index("ctx"), 2) * WIDE, WIDE)
    copies = [
        pltpu.make_async_copy(ref.at[:, pl.ds(begin, WIDE)], own.at[n], sems.at[n])
        for n, ref in enumerate((query, d_out, saved))
    ]
    for copy in copies:
        copy.start()
    for which, source in ((1, swapped), (0, own)):
        if which == 0:
            for copy in copies:
                copy.wait()
        for h in range(GROUP):
            row = which * GROUP + h
            cols = pl.ds(h * HD, HD)
            q_turned[row] = source[0, :, cols].T
            turned = source[1, :, cols].T
            d_turned[row] = turned
            product = turned.astype(jnp.float32) * source[2, :, cols].T.astype(jnp.float32)
            delta[pl.ds(row, 1), :] = jnp.sum(product, axis=0, keepdims=True)


def main_kernel(table, bounds, q_turned, d_turned, delta, *rest):
    near, far = rest[0:4], rest[4:8]
    gq = rest[8:10]
    keep, send = rest[10:14], rest[14:18]
    kv_all, grad_all, gq_all, top, total, lse, gq_out, bias, key_turned, starts, firsts, sems = rest[18:]
    copies = load_blocks(near, far, kv_all, sems, range(4))
    for copy in copies:
        copy.start()
    fill_starts(starts, firsts, table, bounds)
    top[...] = jnp.full(top.shape, HIDE, jnp.float32)
    total[...] = jnp.zeros(total.shape, jnp.float32)
    for copy in copies[:4]:
        copy.wait()

    def add_to_sums(j, carry):
        rel, dc = j // 2, j % 2
        for which in range(2):

            @pl.when(needed(table, firsts, which, j))
            def _():
                fill_bias(bias, starts, table, which, table[0, j])
                k = kv_all[dc, table[4 + dc, rel]]

                def update(h, s):
                    row = which * GROUP + h
                    old, amount = top[row], total[row]
                    for c in range(0, BLOCK, 64):
                        part = (s[c : c + 64] * FACTOR + bias[c : c + 64, :]).reshape(8, 8, BLOCK)
                        new = jnp.maximum(old, fold(jnp.maximum, part))
                        weights = jnp.exp2(part - new[None])
                        amount = amount * jnp.exp2(old - new) + fold(jnp.add, weights)
                        old = new
                    total[row] = amount
                    top[row] = old

                early = {}
                for step in range(GROUP + 1):
                    if step < GROUP:
                        early[step] = dot(k, q_turned[which * GROUP + step], (1, 0))
                    if step >= 1:
                        update(step - 1, early.pop(step - 1))

        return carry

    lax.fori_loop(0, 32, add_to_sums, 0)
    for row in range(2 * GROUP):
        best = jnp.max(top[row], axis=0, keepdims=True)
        amount = jnp.sum(total[row] * jnp.exp2(top[row] - best), axis=0, keepdims=True)
        lse[pl.ds(row, 1), :] = best + jnp.log2(amount)
    gq_all[...] = jnp.zeros(gq_all.shape, jnp.float32)
    for copy in copies[4:]:
        copy.wait()

    def add_gradients(j, carry):
        rel, dc = j // 2, j % 2
        place_k, place_v = table[8 + dc, rel], table[10 + dc, rel]
        any_needed = needed(table, firsts, 0, j) | needed(table, firsts, 1, j)

        @pl.when(jnp.logical_not(any_needed))
        def _():
            grad_all[dc, place_k] = jnp.zeros((BLOCK, HD), jnp.bfloat16)
            grad_all[2 + dc, place_v] = jnp.zeros((BLOCK, HD), jnp.bfloat16)

        @pl.when(any_needed)
        def _():
            key_turned[...] = kv_all[dc, table[4 + dc, rel]].T

        def add_query_block(which, gk_sum, gv_sum):
            fill_bias(bias, starts, table, which, table[0, j])
            k = kv_all[dc, table[4 + dc, rel]]
            v = kv_all[2 + dc, table[6 + dc, rel]]
            turned = key_turned[...]

            def first(h):
                row = which * GROUP + h
                return dot(k, q_turned[row], (1, 0)), dot(v, d_turned[row], (1, 0))

            def middle(h, s, dp):
                row = which * GROUP + h
                p = jnp.exp2(s * FACTOR + bias[...] - lse[pl.ds(row, 1), :])
                ds = (p * (dp - delta[pl.ds(row, 1), :])).astype(jnp.bfloat16)
                return p.astype(jnp.bfloat16), ds

            early, late = {}, {}
            for step in range(GROUP + 2):
                if step < GROUP:
                    early[step] = first(step)
                h = step - 1
                if 0 <= h < GROUP:
                    late[h] = middle(h, *early.pop(h))
                h = step - 2
                if 0 <= h < GROUP:
                    row = which * GROUP + h
                    p, ds = late.pop(h)
                    gv_sum = gv_sum + dot(d_turned[row], p, (1, 1))
                    gk_sum = gk_sum + dot(q_turned[row], ds, (1, 1))
                    gq_all[row] += dot(turned, ds, (1, 0))
            return gk_sum, gv_sum

        zero = jnp.zeros((HD, BLOCK), jnp.float32)
        sums = (zero, zero)
        for which in range(2):
            sums = lax.cond(
                needed(table, firsts, which, j),
                lambda a, b: add_query_block(which, a, b),
                lambda a, b: (a, b),
                *sums,
            )

        @pl.when(any_needed)
        def _():
            grad_all[dc, place_k] = (sums[0] * SCALE).T.astype(jnp.bfloat16)
            grad_all[2 + dc, place_v] = sums[1].T.astype(jnp.bfloat16)

        return carry

    lax.fori_loop(0, 32, add_gradients, 0)
    outs = []
    for n in range(4):
        outs.append(pltpu.make_async_copy(grad_all.at[n, pl.ds(8, 8)], send[n], sems.at[2 * n + 1]))
        outs.append(pltpu.make_async_copy(grad_all.at[n, pl.ds(0, 8)], keep[n], sems.at[2 * n]))
    for copy in outs:
        copy.start()
    for which in (1, 0):
        for h in range(GROUP):
            turned = (gq_all[which * GROUP + h] * SCALE).T.astype(jnp.bfloat16)
            gq_out[which, :, pl.ds(h * HD, HD)] = turned
        outs.append(pltpu.make_async_copy(gq_out.at[which], gq[which], sems.at[8 + which]))
        outs[-1].start()
    for copy in outs:
        copy.wait()


SMEM = pl.BlockSpec(memory_space=pltpu.SMEM)
VMEM = pl.BlockSpec(memory_space=pltpu.VMEM)
ANY = pl.BlockSpec(memory_space=pl.ANY)
TURNED = jax.ShapeDtypeStruct((2 * GROUP, HD, BLOCK), jnp.bfloat16)


def pack_keys(placement, doc_ids, keys, values):
    half = jax.ShapeDtypeStruct((BLOCK, HD), jnp.bfloat16)
    return pl.pallas_call(
        pack_keys_kernel,
        out_shape=[half] * 4 + [jax.ShapeDtypeStruct((1, HD), jnp.int32)],
        in_specs=[SMEM, VMEM, ANY, ANY],
        out_specs=[VMEM] * 5,
        scratch_shapes=[pltpu.SemaphoreType.DMA((4,))],
        cost_estimate=pl.CostEstimate(flops=1000, bytes_accessed=1 << 19, transcendentals=0),
        name="pack_keys",
    )(placement, doc_ids, keys, values)


def pack_queries(query, d_out, saved):
    return pl.pallas_call(
        pack_queries_kernel,
        out_shape=jax.ShapeDtypeStruct((3, BLOCK, WIDE), jnp.bfloat16),
        in_specs=[ANY] * 3,
        out_specs=VMEM,
        scratch_shapes=[pltpu.SemaphoreType.DMA((3,))],
        cost_estimate=pl.CostEstimate(flops=1000, bytes_accessed=3 << 20, transcendentals=0),
        name="pack_queries",
    )(query, d_out, saved)


def prepare(query, d_out, saved, swapped, after):
    return pl.pallas_call(
        prepare_kernel,
        out_shape=[TURNED, TURNED, jax.ShapeDtypeStruct((2 * GROUP, BLOCK), jnp.float32)],
        in_specs=[ANY] * 3 + [VMEM, ANY],
        out_specs=[VMEM] * 3,
        scratch_shapes=[pltpu.VMEM((3, BLOCK, WIDE), jnp.bfloat16), pltpu.SemaphoreType.DMA((3,))],
        compiler_params=pltpu.CompilerParams(vmem_limit_bytes=16 * 1024 * 1024),
        cost_estimate=pl.CostEstimate(flops=2_000_000, bytes_accessed=5 << 20, transcendentals=0),
        name="prepare",
    )(query, d_out, saved, swapped, after)


def gradients(table, bounds, q_turned, d_turned, delta, near, far):
    part = jax.ShapeDtypeStruct((8, BLOCK, HD), jnp.bfloat16)
    return pl.pallas_call(
        main_kernel,
        out_shape=[jax.ShapeDtypeStruct((BLOCK, WIDE), jnp.bfloat16)] * 2 + [part] * 8,
        in_specs=[SMEM] * 2 + [VMEM] * 3 + [ANY] * 8,
        out_specs=[ANY, pl.BlockSpec(memory_space=pltpu.HBM)] + [ANY] * 4 + [pl.BlockSpec(memory_space=pltpu.HBM)] * 4,
        scratch_shapes=[
            pltpu.VMEM((4, 16, BLOCK, HD), jnp.bfloat16),
            pltpu.VMEM((4, 16, BLOCK, HD), jnp.bfloat16),
            pltpu.VMEM((2 * GROUP, HD, BLOCK), jnp.float32),
            pltpu.VMEM((2 * GROUP, 8, BLOCK), jnp.float32),
            pltpu.VMEM((2 * GROUP, 8, BLOCK), jnp.float32),
            pltpu.VMEM((2 * GROUP, BLOCK), jnp.float32),
            pltpu.VMEM((2, BLOCK, WIDE), jnp.bfloat16),
            pltpu.VMEM((BLOCK, BLOCK), jnp.float32),
            pltpu.VMEM((HD, BLOCK), jnp.bfloat16),
            pltpu.VMEM((8, BLOCK), jnp.int32),
            pltpu.SMEM((2,), jnp.int32),
            pltpu.SemaphoreType.DMA((10,)),
        ],
        compiler_params=pltpu.CompilerParams(vmem_limit_bytes=30 * 1024 * 1024),
        cost_estimate=pl.CostEstimate(flops=12_000_000_000, bytes_accessed=10 << 20, transcendentals=16 << 20),
        name="gradients",
    )(table, bounds, q_turned, d_turned, delta, *near, *far)


def gather(parts, edges):
    held = [part[None] for part in parts]
    for step in range(4):
        sent = list(held)
        rows = jnp.broadcast_to(pack_edges(edges)[None], (held[0].shape[0], STAT_ROWS, HD))
        sent[0] = jnp.concatenate([held[0], rows], axis=1)
        come = [across(sent[n], (n + step) % 4) for n in (1, 2, 3, 0)]
        come = come[3:] + come[:3]
        edges = jnp.maximum(edges, unpack_edges(come[0]))
        if step == 3:
            return held, come, edges
        come[0] = come[0][:, :BLOCK]
        held = lax.optimization_barrier([jnp.concatenate(pair, axis=0) for pair in zip(held, come)])


def pack_edges(edges):
    spare = jnp.zeros((STAT_ROWS - 2, HD), jnp.int32)
    return jnp.concatenate([edges // 128, edges % 128, spare], axis=0).astype(jnp.bfloat16)


def unpack_edges(array):
    rows = array[:1, BLOCK : BLOCK + 2].astype(jnp.float32)
    return (rows[:, 0] * 128 + rows[:, 1]).astype(jnp.int32)


def reduce(keep, send):
    for step in range(4):
        if step == 3:
            moved = swap(jnp.stack([keep[1], keep[3]]))
            keep = [keep[0], moved[0], keep[2], moved[1]]
        come = [across(array, (n + step) % 4, n % 2 if step == 3 else 0) for n, array in enumerate(send)]
        total = [
            (a.astype(jnp.float32) + b.astype(jnp.float32)).astype(jnp.bfloat16) for a, b in zip(keep, come)
        ]
        if step == 3:
            return [a[0] for a in total]
        half = total[0].shape[0] // 2
        keep, send = [a[:half] for a in total], [a[half:] for a in total]


def shards(query, keys, values, out_saved, d_out, doc_ids, placement, block_keys):
    me = lax.axis_index("ctx")
    core = me % 2
    z, y = me // 8, (me // 2) % 4

    k_mine, v_mine, k_other, v_other, edges = pack_keys(placement, doc_ids[None], keys, values)
    k_swap, v_swap = swap(k_other), swap(v_other)
    for_x = [lax.ppermute(edges, "head", [(i, (i + r) % 4) for i in range(4)]) for r in (1, 2, 3)]
    edges = jnp.maximum(jnp.maximum(edges, for_x[0]), jnp.maximum(for_x[1], for_x[2]))
    edges = jnp.maximum(edges, swap(edges))
    query, d_out, out_saved, _ = lax.optimization_barrier((query, d_out, out_saved, k_other))
    swapped = swap(pack_queries(query, d_out, out_saved))

    near, far, bounds = gather([k_mine, k_swap, v_mine, v_swap], edges)
    turned = prepare(query, d_out, out_saved, swapped, near[1])

    j = jnp.arange(32)
    slots = index_of((gray(z) * 4 + gray(y)) ^ (j // 2), core ^ (j % 2))
    block_of = jnp.sum(jnp.where(slots[:, None] == jnp.arange(32)[None, :], placement[None, :], 0), axis=1)
    own = block_of[:2]
    chosen = jnp.sum(jnp.where(own[:, None, None] == jnp.arange(32)[None, :, None], block_keys[None], 0), axis=1)
    listed = jnp.any(chosen[:, :, None] == block_of[None, None, :], axis=1).astype(jnp.int32)
    bits = [[(rel >> bit) & 1 for bit in range(4)] for rel in range(32)]
    gathered = [[sum(b[(n + k) % 4] << k for k in range(4)) for b in bits] for n in range(4)]
    reduced = [[sum(b[(n + k) % 4] << (3 - k) for k in range(4)) for b in bits] for n in range(4)]
    table = jnp.concatenate(
        [block_of[None], listed, block_of[None], jnp.array(gathered), jnp.array(reduced)], axis=0
    ).astype(jnp.int32)

    outs = gradients(table, bounds, *turned, near, far)
    gq_mine, gq_other, keep, send = outs[0], outs[1], outs[2:6], outs[6:10]

    gk_mine, gk_other, gv_mine, gv_other = reduce(keep, send)
    gq_swap = swap(gq_other)

    def join(mine, other):
        return jnp.where(
            core == 0, jnp.concatenate([mine, other], axis=1), jnp.concatenate([other, mine], axis=1)
        )

    return (
        join(gq_mine, gq_swap),
        join(gk_mine, gk_other),
        join(gv_mine, gv_other),
    )


def solution(mesh):
    placed = (
        P("ctx", "head"),
        P("ctx", "head"),
        P("ctx", "head"),
        P("ctx", "head"),
        P("ctx", "head"),
        P(("ctx", "head")),
        P(),
        P(),
    )
    return jax.shard_map(
        shards,
        mesh=mesh,
        in_specs=placed,
        out_specs=(P("ctx", "head"), P("ctx", "head"), P("ctx", "head")),
        check_vma=False,
    )
```

```python
import math

import jax
import jax.numpy as jnp
from jax import lax
from jax.experimental import pallas as pl
from jax.experimental.pallas import tpu as pltpu
from jax.sharding import PartitionSpec as P

HD = 128
BLOCK = 256
GROUP = 8
WIDE = GROUP * HD
SCALE = 1.0 / math.sqrt(HD)
FACTOR = SCALE * math.log2(math.e)
HIDE = -1e30
STAT_ROWS = 16
SMALL_QUERY = 240.0


def gray(n):
    return n ^ (n >> 1)


def index_of(corner, core):
    return (gray(corner >> 2) * 4 + gray(corner & 3)) * 2 + core


def across(array, bit, turn=0):
    pairs = [(index_of(n, core), index_of(n ^ (1 << bit), core ^ turn)) for n in range(16) for core in range(2)]
    return lax.ppermute(array, "ctx", pairs)


def swap(array):
    return lax.ppermute(array, "ctx", [(i, i ^ 1) for i in range(32)])


def dot(a, b, contract):
    return lax.dot_general(a, b, ((contract[:1], contract[1:]), ((), ())), preferred_element_type=jnp.float32)


def fold(op, array):
    while array.shape[0] > 1:
        half = array.shape[0] // 2
        array = op(array[:half], array[half:])
    return array[0]


def fill_bias(bias, starts, table, which, key_block):
    key_pos = key_block * BLOCK + lax.broadcasted_iota(jnp.int32, (BLOCK, BLOCK), 0)
    query_pos = table[3, which] * BLOCK + lax.broadcasted_iota(jnp.int32, (1, BLOCK), 1)
    seen = (key_pos >= starts[pl.ds(which, 1), :]) & (key_pos <= query_pos)
    bias[...] = jnp.where(seen, 0.0, HIDE)


def fill_starts(starts, firsts, table, bounds):
    for which in range(2):
        begin = table[3, which] * BLOCK
        pos = begin + lax.broadcasted_iota(jnp.int32, (1, BLOCK), 1)
        row = jnp.zeros((1, BLOCK), jnp.int32)
        first = jnp.int32(0)
        for k in range(4):
            edge = bounds[0, k]
            row = jnp.maximum(row, jnp.where(pos >= edge, edge, 0))
            first = jnp.maximum(first, jnp.where(begin >= edge, edge, 0))
        starts[pl.ds(which, 1), :] = row
        firsts[which] = first


def needed(table, firsts, which, j):
    return (table[1 + which, j] > 0) & (table[0, j] * BLOCK + BLOCK - 1 >= firsts[which])


def block_at(place):
    return pl.ds(pl.multiple_of(place * BLOCK, BLOCK), BLOCK)


def add_to_sums(table, firsts, small, places, keys, bias, starts, top, total, q_turned):
    def masked(s, c):
        return (s[c : c + 64] * FACTOR + bias[c : c + 64, :]).reshape(8, 8, BLOCK)

    def update_small(row, s):
        amount = total[row]
        for c in range(0, BLOCK, 64):
            amount = amount + fold(jnp.add, jnp.exp2(masked(s, c)))
        total[row] = amount

    def update_any(row, s):
        old, amount = top[row], total[row]
        for c in range(0, BLOCK, 64):
            part = masked(s, c)
            new = jnp.maximum(old, fold(jnp.maximum, part))
            weights = jnp.exp2(part - new[None])
            amount = amount * jnp.exp2(old - new) + fold(jnp.add, weights)
            old = new
        total[row] = amount
        top[row] = old

    def run(update):
        def one(t, carry):
            place, dc, which = places.start + t // 4, (t // 2) % 2, t % 2
            j = table[12 + dc, place] * 2 + dc

            @pl.when(needed(table, firsts, which, j))
            def _():
                fill_bias(bias, starts, table, which, table[0, j])
                k = keys[dc, block_at(place), :]
                early = {}
                for step in range(GROUP + 1):
                    if step < GROUP:
                        early[step] = dot(k, q_turned[which * GROUP + step], (1, 0))
                    if step >= 1:
                        update(which * GROUP + step - 1, early.pop(step - 1))

            return carry

        lax.fori_loop(0, 4 * len(places), one, 0)

    pl.when(small[0] == 1)(lambda: run(update_small))
    pl.when(small[0] == 0)(lambda: run(update_any))


def near_sums_kernel(
    table, bounds, small, q_turned, held0, held1, come0, come1, top, total, keys, bias, starts, firsts, sems
):
    half = 4 * BLOCK
    copies = [
        pltpu.make_async_copy(ref, keys.at[n % 2, pl.ds(n // 2 * half, half)], sems.at[n])
        for n, ref in enumerate((held0, held1, come0, come1))
    ]
    for copy in copies:
        copy.start()
    fill_starts(starts, firsts, table, bounds)
    top[...] = jnp.full(top.shape, jnp.where(small[0] == 1, 0.0, HIDE), jnp.float32)
    total[...] = jnp.zeros(total.shape, jnp.float32)
    for copy in copies:
        copy.wait()
    add_to_sums(table, firsts, small, range(8), keys, bias, starts, top, total, q_turned)


def pack_keys_kernel(placement, doc_ids, keys, values, k_mine, v_mine, k_other, v_other, edges, sems):
    me = lax.axis_index("ctx")
    core = lax.rem(me, 2)
    copies = []
    for n, (ref, mine, other) in enumerate(((keys, k_mine, k_other), (values, v_mine, v_other))):
        for part, (out, head) in enumerate(((other, 1 - core), (mine, core))):
            cols = pl.ds(pl.multiple_of(head * HD, HD), HD)
            copies.append(pltpu.make_async_copy(ref.at[:, cols], out, sems.at[2 * n + part]))
    for copy in copies:
        copy.start()
    begin = placement[me] * BLOCK + lax.axis_index("head") * 64
    lane = lax.broadcasted_iota(jnp.int32, (1, HD), 1)
    row = jnp.zeros((1, HD), jnp.int32)
    for k in range(4):
        count = jnp.sum((doc_ids[...] <= k).astype(jnp.int32), axis=1, keepdims=True)
        row = jnp.where(lane == k, jnp.where(count > 0, begin + count, 0), row)
    edges[...] = row
    for copy in copies:
        copy.wait()


def pack_queries_kernel(query, d_out, saved, other, sems):
    core = lax.rem(lax.axis_index("ctx"), 2)
    cols = pl.ds(pl.multiple_of((1 - core) * WIDE, WIDE), WIDE)
    copies = [
        pltpu.make_async_copy(ref.at[:, cols], other.at[n], sems.at[n])
        for n, ref in enumerate((query, d_out, saved))
    ]
    for copy in copies:
        copy.start()
    for copy in copies:
        copy.wait()


def prepare_kernel(query, d_out, saved, swapped, after, q_turned, d_turned, delta, small, own, sems):
    del after
    peak = jnp.zeros((1, BLOCK), jnp.float32)
    begin = pl.multiple_of(lax.rem(lax.axis_index("ctx"), 2) * WIDE, WIDE)
    copies = [
        pltpu.make_async_copy(ref.at[:, pl.ds(begin, WIDE)], own.at[n], sems.at[n])
        for n, ref in enumerate((query, d_out, saved))
    ]
    for copy in copies:
        copy.start()
    for which, source in ((1, swapped), (0, own)):
        if which == 0:
            for copy in copies:
                copy.wait()
        for h in range(GROUP):
            row = which * GROUP + h
            cols = pl.ds(h * HD, HD)
            turned = source[0, :, cols].T
            q_turned[row] = turned
            turned = turned.astype(jnp.float32)
            peak = jnp.maximum(peak, jnp.sum(turned * turned, axis=0, keepdims=True))
            turned = source[1, :, cols].T
            d_turned[row] = turned
            product = turned.astype(jnp.float32) * source[2, :, cols].T.astype(jnp.float32)
            delta[pl.ds(row, 1), :] = jnp.sum(product, axis=0, keepdims=True)
    small[0] = (jnp.max(peak) <= SMALL_QUERY).astype(jnp.int32)


def main_kernel(table, bounds, small, q_turned, d_turned, delta, top_near, total_near, *rest):
    gq = rest[16:18]
    keep, send = rest[18:22], rest[22:26]
    kv_all, grad_all, gq_all, top, total, lse, gq_out, held_sums, bias, key_turned, starts, firsts, sems = rest[26:]
    copies = [
        pltpu.make_async_copy(
            rest[4 * part + n].at[pl.ds(0, 4 * BLOCK)],
            kv_all.at[n, pl.ds(4 * part * BLOCK, 4 * BLOCK)],
            sems.at[4 * part + n],
        )
        for part in range(4)
        for n in range(4)
    ]
    early = (8, 9, 12, 13)
    for n in early:
        copies[n].start()
    for n in range(16):
        if n not in early:
            copies[n].start()
    fill_starts(starts, firsts, table, bounds)
    top[...] = top_near[...]
    total[...] = total_near[...]
    gq_all[...] = jnp.zeros(gq_all.shape, jnp.float32)
    grad_all[...] = jnp.zeros(grad_all.shape, jnp.bfloat16)
    for n in early:
        copies[n].wait()

    add_to_sums(table, firsts, small, range(8, 16), kv_all, bias, starts, top, total, q_turned)
    for row in range(2 * GROUP):
        best = jnp.max(top[row], axis=0, keepdims=True)
        amount = jnp.sum(total[row] * jnp.exp2(top[row] - best), axis=0, keepdims=True)
        lse[pl.ds(row, 1), :] = best + jnp.log2(amount)
    for n in range(16):
        if n not in early:
            copies[n].wait()

    def add_gradients(t, carry):
        j, which = t // 2, t % 2
        rel, dc = j // 2, j % 2

        @pl.when(needed(table, firsts, which, j))
        def _():
            again = (which == 1) & needed(table, firsts, 0, j)
            fill_bias(bias, starts, table, which, table[0, j])
            k = kv_all[dc, block_at(table[4 + dc, rel]), :]
            v = kv_all[2 + dc, block_at(table[6 + dc, rel]), :]

            @pl.when(jnp.logical_not(again))
            def _():
                key_turned[...] = k.T
                held_sums[...] = jnp.zeros(held_sums.shape, jnp.float32)

            turned = key_turned[...]

            def first(h):
                row = which * GROUP + h
                return dot(k, q_turned[row], (1, 0)), dot(v, d_turned[row], (1, 0))

            def middle(h, s, dp):
                row = which * GROUP + h
                p = jnp.exp2(s * FACTOR + bias[...] - lse[pl.ds(row, 1), :])
                ds = (p * (dp - delta[pl.ds(row, 1), :])).astype(jnp.bfloat16)
                return p.astype(jnp.bfloat16), ds

            early, late = {}, {}
            gk_sum, gv_sum = held_sums[0], held_sums[1]
            for step in range(GROUP + 2):
                if step < GROUP:
                    early[step] = first(step)
                h = step - 1
                if 0 <= h < GROUP:
                    late[h] = middle(h, *early.pop(h))
                h = step - 2
                if 0 <= h < GROUP:
                    row = which * GROUP + h
                    p, ds = late.pop(h)
                    gv_sum = gv_sum + dot(d_turned[row], p, (1, 1))
                    gk_sum = gk_sum + dot(q_turned[row], ds, (1, 1))
                    gq_all[row] += dot(turned, ds, (1, 0))
            held_sums[0], held_sums[1] = gk_sum, gv_sum
            grad_all[dc, table[8 + dc, rel]] = (gk_sum * SCALE).T.astype(jnp.bfloat16)
            grad_all[2 + dc, table[10 + dc, rel]] = gv_sum.T.astype(jnp.bfloat16)

        return carry

    lax.fori_loop(0, 64, add_gradients, 0)
    outs = []
    for n in range(4):
        outs.append(pltpu.make_async_copy(grad_all.at[n, pl.ds(8, 8)], send[n], sems.at[2 * n + 1]))
        outs.append(pltpu.make_async_copy(grad_all.at[n, pl.ds(0, 8)], keep[n], sems.at[2 * n]))
    for copy in outs:
        copy.start()
    for which in (1, 0):
        for h in range(GROUP):
            turned = (gq_all[which * GROUP + h] * SCALE).T.astype(jnp.bfloat16)
            gq_out[which, :, pl.ds(h * HD, HD)] = turned
        outs.append(pltpu.make_async_copy(gq_out.at[which], gq[which], sems.at[8 + which]))
        outs[-1].start()
    for copy in outs:
        copy.wait()


SMEM = pl.BlockSpec(memory_space=pltpu.SMEM)
VMEM = pl.BlockSpec(memory_space=pltpu.VMEM)
ANY = pl.BlockSpec(memory_space=pl.ANY)
HBM = pl.BlockSpec(memory_space=pltpu.HBM)
TURNED = jax.ShapeDtypeStruct((2 * GROUP, HD, BLOCK), jnp.bfloat16)


def in_hbm(*arrays):
    return [pltpu.with_memory_space_constraint(array, pltpu.HBM) for array in arrays]


def pack_keys(placement, doc_ids, keys, values):
    half = jax.ShapeDtypeStruct((BLOCK, HD), jnp.bfloat16)
    return pl.pallas_call(
        pack_keys_kernel,
        out_shape=[half] * 4 + [jax.ShapeDtypeStruct((1, HD), jnp.int32)],
        in_specs=[SMEM, VMEM, ANY, ANY],
        out_specs=[VMEM] * 5,
        scratch_shapes=[pltpu.SemaphoreType.DMA((4,))],
        cost_estimate=pl.CostEstimate(flops=1000, bytes_accessed=1 << 19, transcendentals=0),
        name="pack_keys",
    )(placement, doc_ids, keys, values)


def pack_queries(query, d_out, saved):
    return pl.pallas_call(
        pack_queries_kernel,
        out_shape=jax.ShapeDtypeStruct((3, BLOCK, WIDE), jnp.bfloat16),
        in_specs=[ANY] * 3,
        out_specs=VMEM,
        scratch_shapes=[pltpu.SemaphoreType.DMA((3,))],
        cost_estimate=pl.CostEstimate(flops=1000, bytes_accessed=3 << 20, transcendentals=0),
        name="pack_queries",
    )(*in_hbm(query, d_out, saved))


def prepare(query, d_out, saved, swapped, after):
    return pl.pallas_call(
        prepare_kernel,
        out_shape=[
            TURNED,
            TURNED,
            jax.ShapeDtypeStruct((2 * GROUP, BLOCK), jnp.float32),
            jax.ShapeDtypeStruct((1,), jnp.int32),
        ],
        in_specs=[ANY] * 3 + [VMEM, ANY],
        out_specs=[VMEM] * 3 + [SMEM],
        scratch_shapes=[pltpu.VMEM((3, BLOCK, WIDE), jnp.bfloat16), pltpu.SemaphoreType.DMA((3,))],
        compiler_params=pltpu.CompilerParams(vmem_limit_bytes=16 * 1024 * 1024),
        cost_estimate=pl.CostEstimate(flops=2_000_000, bytes_accessed=5 << 20, transcendentals=0),
        name="prepare",
    )(*in_hbm(query, d_out, saved), swapped, after)


def near_sums(table, bounds, small, q_turned, held, come):
    state = jax.ShapeDtypeStruct((2 * GROUP, 8, BLOCK), jnp.float32)
    return pl.pallas_call(
        near_sums_kernel,
        out_shape=[state, state],
        in_specs=[SMEM] * 3 + [VMEM] + [ANY] * 4,
        out_specs=[VMEM] * 2,
        scratch_shapes=[
            pltpu.VMEM((2, 8 * BLOCK, HD), jnp.bfloat16),
            pltpu.VMEM((BLOCK, BLOCK), jnp.float32),
            pltpu.VMEM((8, BLOCK), jnp.int32),
            pltpu.SMEM((2,), jnp.int32),
            pltpu.SemaphoreType.DMA((4,)),
        ],
        compiler_params=pltpu.CompilerParams(vmem_limit_bytes=12 * 1024 * 1024),
        cost_estimate=pl.CostEstimate(flops=1_000_000_000, bytes_accessed=2 << 20, transcendentals=8 << 20),
        name="near_sums",
    )(table, bounds, small, q_turned, *held[:2], *come[:2])


def gradients(table, bounds, small, turned, sums, blocks):
    part = jax.ShapeDtypeStruct((8, BLOCK, HD), jnp.bfloat16)
    return pl.pallas_call(
        main_kernel,
        out_shape=[jax.ShapeDtypeStruct((BLOCK, WIDE), jnp.bfloat16)] * 2
        + [part] * 4
        + [pltpu.HBM((8, BLOCK, HD), jnp.bfloat16)] * 4,
        in_specs=[SMEM] * 3 + [VMEM] * 5 + [ANY] * 16,
        out_specs=[ANY] * 6 + [HBM] * 4,
        scratch_shapes=[
            pltpu.VMEM((4, 16 * BLOCK, HD), jnp.bfloat16),
            pltpu.VMEM((4, 16, BLOCK, HD), jnp.bfloat16),
            pltpu.VMEM((2 * GROUP, HD, BLOCK), jnp.float32),
            pltpu.VMEM((2 * GROUP, 8, BLOCK), jnp.float32),
            pltpu.VMEM((2 * GROUP, 8, BLOCK), jnp.float32),
            pltpu.VMEM((2 * GROUP, BLOCK), jnp.float32),
            pltpu.VMEM((2, BLOCK, WIDE), jnp.bfloat16),
            pltpu.VMEM((2, HD, BLOCK), jnp.float32),
            pltpu.VMEM((BLOCK, BLOCK), jnp.float32),
            pltpu.VMEM((HD, BLOCK), jnp.bfloat16),
            pltpu.VMEM((8, BLOCK), jnp.int32),
            pltpu.SMEM((2,), jnp.int32),
            pltpu.SemaphoreType.DMA((16,)),
        ],
        compiler_params=pltpu.CompilerParams(vmem_limit_bytes=30 * 1024 * 1024),
        cost_estimate=pl.CostEstimate(flops=12_000_000_000, bytes_accessed=10 << 20, transcendentals=16 << 20),
        name="gradients",
    )(table, bounds, small, *turned, *sums, *blocks)


def gather(parts, edges):
    held = [part[None] for part in parts]
    for step in range(3):
        sent = list(held)
        if step > 0:
            rows = jnp.broadcast_to(pack_edges(edges)[None], (held[0].shape[0], STAT_ROWS, HD))
            sent[0] = jnp.concatenate([held[0], rows], axis=1)
        come = [across(sent[n], (n + step) % 4) for n in range(4)]
        if step == 0:
            edges = jnp.maximum(edges, across(edges, 0))
        else:
            edges = jnp.maximum(edges, unpack_edges(come[0]))
            come[0] = come[0][:, :BLOCK]
        if step < 2:
            held = [jnp.concatenate(pair, axis=0) for pair in zip(held, come)]
            held = lax.optimization_barrier(held)
    far_held = [across(held[n], (n + 3) % 4) for n in range(4)]
    far_come = [across(come[n], (n + 3) % 4) for n in range(4)]
    edges = jnp.maximum(edges, across(edges, 3))
    return [array.reshape(4 * BLOCK, HD) for array in held + come + far_held + far_come], edges


def pack_edges(edges):
    spare = jnp.zeros((STAT_ROWS - 2, HD), jnp.int32)
    return jnp.concatenate([edges // 128, edges % 128, spare], axis=0).astype(jnp.bfloat16)


def unpack_edges(array):
    rows = array[:1, BLOCK : BLOCK + 2].astype(jnp.float32)
    return (rows[:, 0] * 128 + rows[:, 1]).astype(jnp.int32)


def reduce(keep, send, late):
    for step in range(4):
        if step == 3:
            moved = swap(jnp.stack([keep[1], keep[3]]))
            keep = [keep[0], moved[0], keep[2], moved[1]]
        come = [across(array, (n + step) % 4, n % 2 if step == 3 else 0) for n, array in enumerate(send)]
        total = [
            (a.astype(jnp.float32) + b.astype(jnp.float32)).astype(jnp.bfloat16) for a, b in zip(keep, come)
        ]
        if step == 3:
            return [a[0] for a in total], late
        if step == 1:
            total[3], late = lax.optimization_barrier((total[3], late))
        half = total[0].shape[0] // 2
        keep, send = [a[:half] for a in total], [a[half:] for a in total]


def shards(query, keys, values, out_saved, d_out, doc_ids, placement, block_keys):
    me = lax.axis_index("ctx")
    core = me % 2
    z, y = me // 8, (me // 2) % 4

    k_mine, v_mine, k_other, v_other, edges = pack_keys(placement, doc_ids[None], keys, values)
    k_swap, v_swap = swap(k_other), swap(v_other)
    query, d_out, out_saved, _ = lax.optimization_barrier((query, d_out, out_saved, k_other))
    swapped = swap(pack_queries(query, d_out, out_saved))
    edges, k_swap = lax.optimization_barrier((edges, k_swap))
    for_x = [lax.ppermute(edges, "head", [(i, (i + r) % 4) for i in range(4)]) for r in (1, 2, 3)]
    edges = jnp.maximum(jnp.maximum(edges, for_x[0]), jnp.maximum(for_x[1], for_x[2]))
    edges = jnp.maximum(edges, swap(edges))
    blocks, bounds = gather([k_mine, k_swap, v_mine, v_swap], edges)
    *turned, small = prepare(query, d_out, out_saved, swapped, blocks[1])

    j = jnp.arange(32)
    slots = index_of((gray(z) * 4 + gray(y)) ^ (j // 2), core ^ (j % 2))
    block_of = jnp.sum(jnp.where(slots[:, None] == jnp.arange(32)[None, :], placement[None, :], 0), axis=1)
    own = block_of[:2]
    chosen = jnp.sum(jnp.where(own[:, None, None] == jnp.arange(32)[None, :, None], block_keys[None], 0), axis=1)
    listed = jnp.any(chosen[:, :, None] == block_of[None, None, :], axis=1).astype(jnp.int32)
    bits = [[(rel >> bit) & 1 for bit in range(4)] for rel in range(32)]
    gathered = [[sum(b[(n + k) % 4] << k for k in range(4)) for b in bits] for n in range(4)]
    reduced = [[sum(b[(n + k) % 4] << (3 - k) for k in range(4)) for b in bits] for n in range(4)]
    order = [[gathered[n].index(place % 16) for place in range(32)] for n in range(2)]
    table = jnp.concatenate(
        [block_of[None], listed, block_of[None], jnp.array(gathered), jnp.array(reduced), jnp.array(order)], axis=0
    ).astype(jnp.int32)

    sums = near_sums(table, bounds, small, turned[0], blocks[0:4], blocks[4:8])
    outs = gradients(table, bounds, small, turned, sums, blocks)
    (gk_mine, gk_other, gv_mine, gv_other), gq_other = reduce(outs[2:6], outs[6:10], outs[1])

    def side_by_side(mine, other):
        return jnp.where(
            core == 0, jnp.concatenate([mine, other], axis=1), jnp.concatenate([other, mine], axis=1)
        )

    return (
        side_by_side(outs[0], swap(gq_other)),
        side_by_side(gk_mine, gk_other),
        side_by_side(gv_mine, gv_other),
    )


def solution(mesh):
    placed = (
        P("ctx", "head"),
        P("ctx", "head"),
        P("ctx", "head"),
        P("ctx", "head"),
        P("ctx", "head"),
        P(("ctx", "head")),
        P(),
        P(),
    )
    return jax.shard_map(
        shards,
        mesh=mesh,
        in_specs=placed,
        out_specs=(P("ctx", "head"), P("ctx", "head"), P("ctx", "head")),
        check_vma=False,
    )
```

```python
import math

import jax
import jax.numpy as jnp
from jax import lax
from jax.experimental import pallas as pl
from jax.experimental.pallas import tpu as pltpu
from jax.sharding import PartitionSpec as P

HD = 128
BLOCK = 256
GROUP = 8
WIDE = GROUP * HD
SCALE = 1.0 / math.sqrt(HD)
FACTOR = SCALE * math.log2(math.e)
HIDE = -1e30
STAT_ROWS = 16
SMALL_QUERY = 240.0


def gray(n):
    return n ^ (n >> 1)


def index_of(corner, core):
    return (gray(corner >> 2) * 4 + gray(corner & 3)) * 2 + core


def across(array, bit, turn=0):
    pairs = [(index_of(n, core), index_of(n ^ (1 << bit), core ^ turn)) for n in range(16) for core in range(2)]
    return lax.ppermute(array, "ctx", pairs)


def swap(array):
    return lax.ppermute(array, "ctx", [(i, i ^ 1) for i in range(32)])


def dot(a, b, contract):
    return lax.dot_general(a, b, ((contract[:1], contract[1:]), ((), ())), preferred_element_type=jnp.float32)


def fold(op, array):
    while array.shape[0] > 1:
        half = array.shape[0] // 2
        array = op(array[:half], array[half:])
    return array[0]


def fill_bias(bias, starts, table, which, key_block):
    key_pos = key_block * BLOCK + lax.broadcasted_iota(jnp.int32, (BLOCK, BLOCK), 0)
    query_pos = table[3, which] * BLOCK + lax.broadcasted_iota(jnp.int32, (1, BLOCK), 1)
    seen = (key_pos >= starts[pl.ds(which, 1), :]) & (key_pos <= query_pos)
    bias[...] = jnp.where(seen, 0.0, HIDE)


def fill_starts(starts, firsts, table, bounds):
    for which in range(2):
        begin = table[3, which] * BLOCK
        pos = begin + lax.broadcasted_iota(jnp.int32, (1, BLOCK), 1)
        row = jnp.zeros((1, BLOCK), jnp.int32)
        first = jnp.int32(0)
        for k in range(4):
            edge = bounds[0, k]
            row = jnp.maximum(row, jnp.where(pos >= edge, edge, 0))
            first = jnp.maximum(first, jnp.where(begin >= edge, edge, 0))
        starts[pl.ds(which, 1), :] = row
        firsts[which] = first


def needed(table, firsts, which, j):
    return (table[1 + which, j] > 0) & (table[0, j] * BLOCK + BLOCK - 1 >= firsts[which])


def block_at(place):
    return pl.ds(pl.multiple_of(place * BLOCK, BLOCK), BLOCK)


def add_to_sums(table, firsts, small, places, keys, bias, starts, top, total, q_turned):
    def masked(s, c):
        return (s[c : c + 64] * FACTOR + bias[c : c + 64, :]).reshape(8, 8, BLOCK)

    def update_small(row, s):
        amount = total[row]
        for c in range(0, BLOCK, 64):
            amount = amount + fold(jnp.add, jnp.exp2(masked(s, c)))
        total[row] = amount

    def update_any(row, s):
        old, amount = top[row], total[row]
        for c in range(0, BLOCK, 64):
            part = masked(s, c)
            new = jnp.maximum(old, fold(jnp.maximum, part))
            weights = jnp.exp2(part - new[None])
            amount = amount * jnp.exp2(old - new) + fold(jnp.add, weights)
            old = new
        total[row] = amount
        top[row] = old

    def run(update):
        def one(t, carry):
            place, dc, which = places.start + t // 4, (t // 2) % 2, t % 2
            j = table[12 + dc, place] * 2 + dc

            @pl.when(needed(table, firsts, which, j))
            def _():
                fill_bias(bias, starts, table, which, table[0, j])
                k = keys[dc, block_at(place), :]
                early = {}
                for step in range(GROUP + 1):
                    if step < GROUP:
                        early[step] = dot(k, q_turned[which * GROUP + step], (1, 0))
                    if step >= 1:
                        update(which * GROUP + step - 1, early.pop(step - 1))

            return carry

        lax.fori_loop(0, 4 * len(places), one, 0)

    pl.when(small[0] == 1)(lambda: run(update_small))
    pl.when(small[0] == 0)(lambda: run(update_any))


def near_sums_kernel(
    table, bounds, small, q_turned, held0, held1, come0, come1, top, total, keys, bias, starts, firsts, sems
):
    half = 4 * BLOCK
    copies = [
        pltpu.make_async_copy(ref, keys.at[n % 2, pl.ds(n // 2 * half, half)], sems.at[n])
        for n, ref in enumerate((held0, held1, come0, come1))
    ]
    for copy in copies:
        copy.start()
    fill_starts(starts, firsts, table, bounds)
    top[...] = jnp.full(top.shape, jnp.where(small[0] == 1, 0.0, HIDE), jnp.float32)
    total[...] = jnp.zeros(total.shape, jnp.float32)
    for copy in copies:
        copy.wait()
    add_to_sums(table, firsts, small, range(8), keys, bias, starts, top, total, q_turned)


def pack_keys_kernel(placement, doc_ids, keys, values, k_mine, v_mine, k_other, v_other, edges, sems):
    me = lax.axis_index("ctx")
    core = lax.rem(me, 2)
    copies = []
    for n, (ref, mine, other) in enumerate(((keys, k_mine, k_other), (values, v_mine, v_other))):
        for part, (out, head) in enumerate(((other, 1 - core), (mine, core))):
            cols = pl.ds(pl.multiple_of(head * HD, HD), HD)
            copies.append(pltpu.make_async_copy(ref.at[:, cols], out, sems.at[2 * n + part]))
    for copy in copies:
        copy.start()
    begin = placement[me] * BLOCK + lax.axis_index("head") * 64
    lane = lax.broadcasted_iota(jnp.int32, (1, HD), 1)
    row = jnp.zeros((1, HD), jnp.int32)
    for k in range(4):
        count = jnp.sum((doc_ids[...] <= k).astype(jnp.int32), axis=1, keepdims=True)
        row = jnp.where(lane == k, jnp.where(count > 0, begin + count, 0), row)
    edges[...] = row
    for copy in copies:
        copy.wait()


def pack_queries_kernel(query, d_out, saved, other, sems):
    core = lax.rem(lax.axis_index("ctx"), 2)
    cols = pl.ds(pl.multiple_of((1 - core) * WIDE, WIDE), WIDE)
    copies = [
        pltpu.make_async_copy(ref.at[:, cols], other.at[n], sems.at[n])
        for n, ref in enumerate((query, d_out, saved))
    ]
    for copy in copies:
        copy.start()
    for copy in copies:
        copy.wait()


def prepare_kernel(query, d_out, saved, swapped, after, q_turned, d_turned, delta, small, own, sems):
    del after
    peak = jnp.zeros((1, BLOCK), jnp.float32)
    begin = pl.multiple_of(lax.rem(lax.axis_index("ctx"), 2) * WIDE, WIDE)
    copies = [
        pltpu.make_async_copy(ref.at[:, pl.ds(begin, WIDE)], own.at[n], sems.at[n])
        for n, ref in enumerate((query, d_out, saved))
    ]
    for copy in copies:
        copy.start()
    for which, source in ((1, swapped), (0, own)):
        if which == 0:
            for copy in copies:
                copy.wait()
        for h in range(GROUP):
            row = which * GROUP + h
            cols = pl.ds(h * HD, HD)
            turned = source[0, :, cols].T
            q_turned[row] = turned
            turned = turned.astype(jnp.float32)
            peak = jnp.maximum(peak, jnp.sum(turned * turned, axis=0, keepdims=True))
            turned = source[1, :, cols].T
            d_turned[row] = turned
            product = turned.astype(jnp.float32) * source[2, :, cols].T.astype(jnp.float32)
            delta[pl.ds(row, 1), :] = jnp.sum(product, axis=0, keepdims=True)
    small[0] = (jnp.max(peak) <= SMALL_QUERY).astype(jnp.int32)


def main_kernel(table, bounds, small, q_turned, d_turned, delta, top_near, total_near, *rest):
    gq = rest[16:18]
    keep, send = rest[18:22], rest[22:26]
    kv_all, grad_all, gq_all, top, total, lse, gq_out, held_sums, bias, key_turned, starts, firsts, sems = rest[26:]
    copies = [
        pltpu.make_async_copy(
            rest[4 * part + n].at[pl.ds(0, 4 * BLOCK)],
            kv_all.at[n, pl.ds(4 * part * BLOCK, 4 * BLOCK)],
            sems.at[4 * part + n],
        )
        for part in range(4)
        for n in range(4)
    ]
    early = (8, 9, 12, 13)
    for n in early:
        copies[n].start()
    for n in range(16):
        if n not in early:
            copies[n].start()
    fill_starts(starts, firsts, table, bounds)
    top[...] = top_near[...]
    total[...] = total_near[...]
    gq_all[...] = jnp.zeros(gq_all.shape, jnp.float32)
    grad_all[...] = jnp.zeros(grad_all.shape, jnp.bfloat16)
    for n in early:
        copies[n].wait()

    add_to_sums(table, firsts, small, range(8, 16), kv_all, bias, starts, top, total, q_turned)
    for row in range(2 * GROUP):
        best = jnp.max(top[row], axis=0, keepdims=True)
        amount = jnp.sum(total[row] * jnp.exp2(top[row] - best), axis=0, keepdims=True)
        lse[pl.ds(row, 1), :] = best + jnp.log2(amount)
    for n in range(16):
        if n not in early:
            copies[n].wait()

    def add_gradients(t, carry):
        j, which = t // 2, t % 2
        rel, dc = j // 2, j % 2

        @pl.when(needed(table, firsts, which, j))
        def _():
            again = (which == 1) & needed(table, firsts, 0, j)
            fill_bias(bias, starts, table, which, table[0, j])
            k = kv_all[dc, block_at(table[4 + dc, rel]), :]
            v = kv_all[2 + dc, block_at(table[6 + dc, rel]), :]

            @pl.when(jnp.logical_not(again))
            def _():
                key_turned[...] = k.T
                held_sums[...] = jnp.zeros(held_sums.shape, jnp.float32)

            turned = key_turned[...]

            def first(h):
                row = which * GROUP + h
                return dot(k, q_turned[row], (1, 0)), dot(v, d_turned[row], (1, 0))

            def middle(h, s, dp):
                row = which * GROUP + h
                p = jnp.exp2(s * FACTOR + bias[...] - lse[pl.ds(row, 1), :])
                ds = (p * (dp - delta[pl.ds(row, 1), :])).astype(jnp.bfloat16)
                return p.astype(jnp.bfloat16), ds

            early, late = {}, {}
            gk_sum, gv_sum = held_sums[0], held_sums[1]
            for step in range(GROUP + 2):
                if step < GROUP:
                    early[step] = first(step)
                h = step - 1
                if 0 <= h < GROUP:
                    late[h] = middle(h, *early.pop(h))
                h = step - 2
                if 0 <= h < GROUP:
                    row = which * GROUP + h
                    p, ds = late.pop(h)
                    gv_sum = gv_sum + dot(d_turned[row], p, (1, 1))
                    gk_sum = gk_sum + dot(q_turned[row], ds, (1, 1))
                    gq_all[row] += dot(turned, ds, (1, 0))
            held_sums[0], held_sums[1] = gk_sum, gv_sum
            grad_all[dc, table[8 + dc, rel]] = (gk_sum * SCALE).T.astype(jnp.bfloat16)
            grad_all[2 + dc, table[10 + dc, rel]] = gv_sum.T.astype(jnp.bfloat16)

        return carry

    lax.fori_loop(0, 64, add_gradients, 0)
    outs = []
    for n in range(4):
        outs.append(pltpu.make_async_copy(grad_all.at[n, pl.ds(8, 8)], send[n], sems.at[2 * n + 1]))
        outs.append(pltpu.make_async_copy(grad_all.at[n, pl.ds(0, 8)], keep[n], sems.at[2 * n]))
    for copy in outs:
        copy.start()
    for which in (1, 0):
        for h in range(GROUP):
            turned = (gq_all[which * GROUP + h] * SCALE).T.astype(jnp.bfloat16)
            gq_out[which, :, pl.ds(h * HD, HD)] = turned
        outs.append(pltpu.make_async_copy(gq_out.at[which], gq[which], sems.at[8 + which]))
        outs[-1].start()
    for copy in outs:
        copy.wait()


SMEM = pl.BlockSpec(memory_space=pltpu.SMEM)
VMEM = pl.BlockSpec(memory_space=pltpu.VMEM)
ANY = pl.BlockSpec(memory_space=pl.ANY)
HBM = pl.BlockSpec(memory_space=pltpu.HBM)
TURNED = jax.ShapeDtypeStruct((2 * GROUP, HD, BLOCK), jnp.bfloat16)


def in_hbm(*arrays):
    return [pltpu.with_memory_space_constraint(array, pltpu.HBM) for array in arrays]


def pack_keys(placement, doc_ids, keys, values):
    half = jax.ShapeDtypeStruct((BLOCK, HD), jnp.bfloat16)
    return pl.pallas_call(
        pack_keys_kernel,
        out_shape=[half] * 4 + [jax.ShapeDtypeStruct((1, HD), jnp.int32)],
        in_specs=[SMEM, VMEM, ANY, ANY],
        out_specs=[VMEM] * 5,
        scratch_shapes=[pltpu.SemaphoreType.DMA((4,))],
        cost_estimate=pl.CostEstimate(flops=1000, bytes_accessed=1 << 19, transcendentals=0),
        name="pack_keys",
    )(placement, doc_ids, keys, values)


def pack_queries(query, d_out, saved):
    return pl.pallas_call(
        pack_queries_kernel,
        out_shape=jax.ShapeDtypeStruct((3, BLOCK, WIDE), jnp.bfloat16),
        in_specs=[ANY] * 3,
        out_specs=VMEM,
        scratch_shapes=[pltpu.SemaphoreType.DMA((3,))],
        cost_estimate=pl.CostEstimate(flops=1000, bytes_accessed=3 << 20, transcendentals=0),
        name="pack_queries",
    )(*in_hbm(query, d_out, saved))


def prepare(query, d_out, saved, swapped, after):
    return pl.pallas_call(
        prepare_kernel,
        out_shape=[
            TURNED,
            TURNED,
            jax.ShapeDtypeStruct((2 * GROUP, BLOCK), jnp.float32),
            jax.ShapeDtypeStruct((1,), jnp.int32),
        ],
        in_specs=[ANY] * 3 + [VMEM, ANY],
        out_specs=[VMEM] * 3 + [SMEM],
        scratch_shapes=[pltpu.VMEM((3, BLOCK, WIDE), jnp.bfloat16), pltpu.SemaphoreType.DMA((3,))],
        compiler_params=pltpu.CompilerParams(vmem_limit_bytes=16 * 1024 * 1024),
        cost_estimate=pl.CostEstimate(flops=2_000_000, bytes_accessed=5 << 20, transcendentals=0),
        name="prepare",
    )(*in_hbm(query, d_out, saved), swapped, after)


def near_sums(table, bounds, small, q_turned, held, come):
    state = jax.ShapeDtypeStruct((2 * GROUP, 8, BLOCK), jnp.float32)
    return pl.pallas_call(
        near_sums_kernel,
        out_shape=[state, state],
        in_specs=[SMEM] * 3 + [VMEM] + [ANY] * 4,
        out_specs=[VMEM] * 2,
        scratch_shapes=[
            pltpu.VMEM((2, 8 * BLOCK, HD), jnp.bfloat16),
            pltpu.VMEM((BLOCK, BLOCK), jnp.float32),
            pltpu.VMEM((8, BLOCK), jnp.int32),
            pltpu.SMEM((2,), jnp.int32),
            pltpu.SemaphoreType.DMA((4,)),
        ],
        compiler_params=pltpu.CompilerParams(vmem_limit_bytes=12 * 1024 * 1024),
        cost_estimate=pl.CostEstimate(flops=1_000_000_000, bytes_accessed=2 << 20, transcendentals=8 << 20),
        name="near_sums",
    )(table, bounds, small, q_turned, *held[:2], *come[:2])


def gradients(table, bounds, small, turned, sums, blocks):
    part = jax.ShapeDtypeStruct((8, BLOCK, HD), jnp.bfloat16)
    return pl.pallas_call(
        main_kernel,
        out_shape=[pltpu.HBM((BLOCK, WIDE), jnp.bfloat16)] * 2
        + [part] * 4
        + [pltpu.HBM((8, BLOCK, HD), jnp.bfloat16)] * 4,
        in_specs=[SMEM] * 3 + [VMEM] * 5 + [ANY] * 16,
        out_specs=[HBM] * 2 + [ANY] * 4 + [HBM] * 4,
        scratch_shapes=[
            pltpu.VMEM((4, 16 * BLOCK, HD), jnp.bfloat16),
            pltpu.VMEM((4, 16, BLOCK, HD), jnp.bfloat16),
            pltpu.VMEM((2 * GROUP, HD, BLOCK), jnp.float32),
            pltpu.VMEM((2 * GROUP, 8, BLOCK), jnp.float32),
            pltpu.VMEM((2 * GROUP, 8, BLOCK), jnp.float32),
            pltpu.VMEM((2 * GROUP, BLOCK), jnp.float32),
            pltpu.VMEM((2, BLOCK, WIDE), jnp.bfloat16),
            pltpu.VMEM((2, HD, BLOCK), jnp.float32),
            pltpu.VMEM((BLOCK, BLOCK), jnp.float32),
            pltpu.VMEM((HD, BLOCK), jnp.bfloat16),
            pltpu.VMEM((8, BLOCK), jnp.int32),
            pltpu.SMEM((2,), jnp.int32),
            pltpu.SemaphoreType.DMA((16,)),
        ],
        compiler_params=pltpu.CompilerParams(vmem_limit_bytes=30 * 1024 * 1024),
        cost_estimate=pl.CostEstimate(flops=12_000_000_000, bytes_accessed=10 << 20, transcendentals=16 << 20),
        name="gradients",
    )(table, bounds, small, *turned, *sums, *blocks)


def gather(parts, edges):
    held = [part[None] for part in parts]
    for step in range(3):
        sent = list(held)
        if step > 0:
            rows = jnp.broadcast_to(pack_edges(edges)[None], (held[0].shape[0], STAT_ROWS, HD))
            sent[0] = jnp.concatenate([held[0], rows], axis=1)
        come = [across(sent[n], (n + step) % 4) for n in range(4)]
        if step == 0:
            edges = jnp.maximum(edges, across(edges, 0))
        else:
            edges = jnp.maximum(edges, unpack_edges(come[0]))
            come[0] = come[0][:, :BLOCK]
        if step < 2:
            held = [jnp.concatenate(pair, axis=0) for pair in zip(held, come)]
            held = lax.optimization_barrier(held)
    far_held = [across(held[n], (n + 3) % 4) for n in range(4)]
    far_come = [across(come[n], (n + 3) % 4) for n in range(4)]
    edges = jnp.maximum(edges, across(edges, 3))
    return [array.reshape(4 * BLOCK, HD) for array in held + come + far_held + far_come], edges


def pack_edges(edges):
    spare = jnp.zeros((STAT_ROWS - 2, HD), jnp.int32)
    return jnp.concatenate([edges // 128, edges % 128, spare], axis=0).astype(jnp.bfloat16)


def unpack_edges(array):
    rows = array[:1, BLOCK : BLOCK + 2].astype(jnp.float32)
    return (rows[:, 0] * 128 + rows[:, 1]).astype(jnp.int32)


def reduce(keep, send, gq_mine, gq_other, side_by_side):
    for step in range(4):
        if step == 3:
            moved = swap(jnp.stack([keep[1], keep[3]]))
            keep = [keep[0], moved[0], keep[2], moved[1]]
        come = [across(array, (n + step) % 4, n % 2 if step == 3 else 0) for n, array in enumerate(send)]
        total = [
            (a.astype(jnp.float32) + b.astype(jnp.float32)).astype(jnp.bfloat16) for a, b in zip(keep, come)
        ]
        if step == 3:
            return [a[0] for a in total], gq
        if step == 1:
            total[3], gq_other = lax.optimization_barrier((total[3], gq_other))
            gq = side_by_side(gq_mine, swap(gq_other))
        if step == 2:
            total[3], gq = lax.optimization_barrier((total[3], gq))
        half = total[0].shape[0] // 2
        keep, send = [a[:half] for a in total], [a[half:] for a in total]


def shards(query, keys, values, out_saved, d_out, doc_ids, placement, block_keys):
    me = lax.axis_index("ctx")
    core = me % 2
    z, y = me // 8, (me // 2) % 4

    k_mine, v_mine, k_other, v_other, edges = pack_keys(placement, doc_ids[None], keys, values)
    k_swap, v_swap = swap(k_other), swap(v_other)
    query, d_out, out_saved, _ = lax.optimization_barrier((query, d_out, out_saved, k_other))
    swapped = swap(pack_queries(query, d_out, out_saved))
    edges, k_swap = lax.optimization_barrier((edges, k_swap))
    for_x = [lax.ppermute(edges, "head", [(i, (i + r) % 4) for i in range(4)]) for r in (1, 2, 3)]
    edges = jnp.maximum(jnp.maximum(edges, for_x[0]), jnp.maximum(for_x[1], for_x[2]))
    edges = jnp.maximum(edges, swap(edges))
    blocks, bounds = gather([k_mine, k_swap, v_mine, v_swap], edges)
    *turned, small = prepare(query, d_out, out_saved, swapped, blocks[1])

    j = jnp.arange(32)
    slots = index_of((gray(z) * 4 + gray(y)) ^ (j // 2), core ^ (j % 2))
    block_of = jnp.sum(jnp.where(slots[:, None] == jnp.arange(32)[None, :], placement[None, :], 0), axis=1)
    own = block_of[:2]
    chosen = jnp.sum(jnp.where(own[:, None, None] == jnp.arange(32)[None, :, None], block_keys[None], 0), axis=1)
    listed = jnp.any(chosen[:, :, None] == block_of[None, None, :], axis=1).astype(jnp.int32)
    bits = [[(rel >> bit) & 1 for bit in range(4)] for rel in range(32)]
    gathered = [[sum(b[(n + k) % 4] << k for k in range(4)) for b in bits] for n in range(4)]
    reduced = [[sum(b[(n + k) % 4] << (3 - k) for k in range(4)) for b in bits] for n in range(4)]
    order = [[gathered[n].index(place % 16) for place in range(32)] for n in range(2)]
    table = jnp.concatenate(
        [block_of[None], listed, block_of[None], jnp.array(gathered), jnp.array(reduced), jnp.array(order)], axis=0
    ).astype(jnp.int32)

    sums = near_sums(table, bounds, small, turned[0], blocks[0:4], blocks[4:8])
    outs = gradients(table, bounds, small, turned, sums, blocks)
    def side_by_side(mine, other):
        return jnp.where(
            core == 0, jnp.concatenate([mine, other], axis=1), jnp.concatenate([other, mine], axis=1)
        )

    (gk_mine, gk_other, gv_mine, gv_other), gq = reduce(outs[2:6], outs[6:10], *outs[:2], side_by_side)
    return gq, side_by_side(gk_mine, gk_other), side_by_side(gv_mine, gv_other)


def solution(mesh):
    placed = (
        P("ctx", "head"),
        P("ctx", "head"),
        P("ctx", "head"),
        P("ctx", "head"),
        P("ctx", "head"),
        P(("ctx", "head")),
        P(),
        P(),
    )
    return jax.shard_map(
        shards,
        mesh=mesh,
        in_specs=placed,
        out_specs=(P("ctx", "head"), P("ctx", "head"), P("ctx", "head")),
        check_vma=False,
    )
```

```python
import math

import jax
import jax.numpy as jnp
from jax import lax
from jax.experimental import pallas as pl
from jax.experimental.pallas import tpu as pltpu
from jax.sharding import PartitionSpec as P

HD = 128
BLOCK = 256
GROUP = 8
WIDE = GROUP * HD
SCALE = 1.0 / math.sqrt(HD)
FACTOR = SCALE * math.log2(math.e)
HIDE = -1e30
STAT_ROWS = 16
SMALL_QUERY = 240.0


def gray(n):
    return n ^ (n >> 1)


def index_of(corner, core):
    return (gray(corner >> 2) * 4 + gray(corner & 3)) * 2 + core


def across(array, bit, turn=0):
    pairs = [(index_of(n, core), index_of(n ^ (1 << bit), core ^ turn)) for n in range(16) for core in range(2)]
    return lax.ppermute(array, "ctx", pairs)


def swap(array):
    return lax.ppermute(array, "ctx", [(i, i ^ 1) for i in range(32)])


def dot(a, b, contract):
    return lax.dot_general(a, b, ((contract[:1], contract[1:]), ((), ())), preferred_element_type=jnp.float32)


def fold(op, array):
    while array.shape[0] > 1:
        half = array.shape[0] // 2
        array = op(array[:half], array[half:])
    return array[0]


def fill_bias(bias, starts, table, which, key_block):
    key_pos = key_block * BLOCK + lax.broadcasted_iota(jnp.int32, (BLOCK, BLOCK), 0)
    query_pos = table[3, which] * BLOCK + lax.broadcasted_iota(jnp.int32, (1, BLOCK), 1)
    seen = (key_pos >= starts[pl.ds(which, 1), :]) & (key_pos <= query_pos)
    bias[...] = jnp.where(seen, 0.0, HIDE)


def fill_starts(starts, firsts, table, bounds):
    for which in range(2):
        begin = table[3, which] * BLOCK
        pos = begin + lax.broadcasted_iota(jnp.int32, (1, BLOCK), 1)
        row = jnp.zeros((1, BLOCK), jnp.int32)
        first = jnp.int32(0)
        for k in range(4):
            edge = bounds[0, k]
            row = jnp.maximum(row, jnp.where(pos >= edge, edge, 0))
            first = jnp.maximum(first, jnp.where(begin >= edge, edge, 0))
        starts[pl.ds(which, 1), :] = row
        firsts[which] = first


def needed(table, firsts, which, j):
    return (table[1 + which, j] > 0) & (table[0, j] * BLOCK + BLOCK - 1 >= firsts[which])


def block_at(place):
    return pl.ds(pl.multiple_of(place * BLOCK, BLOCK), BLOCK)


def add_to_sums(table, firsts, small, places, keys, bias, starts, top, total, q_turned):
    def masked(s, c):
        return (s[c : c + 64] * FACTOR + bias[c : c + 64, :]).reshape(8, 8, BLOCK)

    def update_small(row, s):
        amount = total[row]
        for c in range(0, BLOCK, 64):
            amount = amount + fold(jnp.add, jnp.exp2(masked(s, c)))
        total[row] = amount

    def update_any(row, s):
        old, amount = top[row], total[row]
        for c in range(0, BLOCK, 64):
            part = masked(s, c)
            new = jnp.maximum(old, fold(jnp.maximum, part))
            weights = jnp.exp2(part - new[None])
            amount = amount * jnp.exp2(old - new) + fold(jnp.add, weights)
            old = new
        total[row] = amount
        top[row] = old

    def run(update):
        def one(t, carry):
            place, dc, which = places.start + t // 4, (t // 2) % 2, t % 2
            j = table[12 + dc, place] * 2 + dc

            @pl.when(needed(table, firsts, which, j))
            def _():
                fill_bias(bias, starts, table, which, table[0, j])
                k = keys[dc, block_at(place), :]
                early = {}
                for step in range(GROUP + 1):
                    if step < GROUP:
                        early[step] = dot(k, q_turned[which * GROUP + step], (1, 0))
                    if step >= 1:
                        update(which * GROUP + step - 1, early.pop(step - 1))

            return carry

        lax.fori_loop(0, 4 * len(places), one, 0)

    pl.when(small[0] == 1)(lambda: run(update_small))
    pl.when(small[0] == 0)(lambda: run(update_any))


def near_sums_kernel(
    table, bounds, small, q_turned, held0, held1, come0, come1, top, total, keys, bias, starts, firsts, sems
):
    half = 4 * BLOCK
    copies = [
        pltpu.make_async_copy(ref, keys.at[n % 2, pl.ds(n // 2 * half, half)], sems.at[n])
        for n, ref in enumerate((held0, held1, come0, come1))
    ]
    for copy in copies:
        copy.start()
    fill_starts(starts, firsts, table, bounds)
    top[...] = jnp.full(top.shape, jnp.where(small[0] == 1, 0.0, HIDE), jnp.float32)
    total[...] = jnp.zeros(total.shape, jnp.float32)
    for copy in copies:
        copy.wait()
    add_to_sums(table, firsts, small, range(8), keys, bias, starts, top, total, q_turned)


def pack_keys_kernel(placement, doc_ids, keys, values, k_mine, v_mine, k_other, v_other, edges, sems):
    me = lax.axis_index("ctx")
    core = lax.rem(me, 2)
    copies = []
    for n, (ref, mine, other) in enumerate(((keys, k_mine, k_other), (values, v_mine, v_other))):
        for part, (out, head) in enumerate(((other, 1 - core), (mine, core))):
            cols = pl.ds(pl.multiple_of(head * HD, HD), HD)
            copies.append(pltpu.make_async_copy(ref.at[:, cols], out, sems.at[2 * n + part]))
    for copy in copies:
        copy.start()
    begin = placement[me] * BLOCK + lax.axis_index("head") * 64
    lane = lax.broadcasted_iota(jnp.int32, (1, HD), 1)
    row = jnp.zeros((1, HD), jnp.int32)
    for k in range(4):
        count = jnp.sum((doc_ids[...] <= k).astype(jnp.int32), axis=1, keepdims=True)
        row = jnp.where(lane == k, jnp.where(count > 0, begin + count, 0), row)
    edges[...] = row
    for copy in copies:
        copy.wait()


def pack_queries_kernel(query, d_out, saved, other, sems):
    core = lax.rem(lax.axis_index("ctx"), 2)
    cols = pl.ds(pl.multiple_of((1 - core) * WIDE, WIDE), WIDE)
    copies = [
        pltpu.make_async_copy(ref.at[:, cols], other.at[n], sems.at[n])
        for n, ref in enumerate((query, d_out, saved))
    ]
    for copy in copies:
        copy.start()
    for copy in copies:
        copy.wait()


def prepare_kernel(query, d_out, saved, swapped, after, q_turned, d_turned, delta, small, own, sems):
    del after
    peak = jnp.zeros((1, BLOCK), jnp.float32)
    begin = pl.multiple_of(lax.rem(lax.axis_index("ctx"), 2) * WIDE, WIDE)
    copies = [
        pltpu.make_async_copy(ref.at[:, pl.ds(begin, WIDE)], own.at[n], sems.at[n])
        for n, ref in enumerate((query, d_out, saved))
    ]
    for copy in copies:
        copy.start()
    for which, source in ((1, swapped), (0, own)):
        if which == 0:
            for copy in copies:
                copy.wait()
        for h in range(GROUP):
            row = which * GROUP + h
            cols = pl.ds(h * HD, HD)
            turned = source[0, :, cols].T
            q_turned[row] = turned
            turned = turned.astype(jnp.float32)
            peak = jnp.maximum(peak, jnp.sum(turned * turned, axis=0, keepdims=True))
            turned = source[1, :, cols].T
            d_turned[row] = turned
            product = turned.astype(jnp.float32) * source[2, :, cols].T.astype(jnp.float32)
            delta[pl.ds(row, 1), :] = jnp.sum(product, axis=0, keepdims=True)
    small[0] = (jnp.max(peak) <= SMALL_QUERY).astype(jnp.int32)


def main_kernel(table, bounds, small, q_turned, d_turned, delta, top_near, total_near, *rest):
    gq = rest[16:18]
    keep, send = rest[18:22], rest[22:26]
    kv_all, grad_all, gq_all, top, total, lse, gq_out, held_sums, bias, key_turned, starts, firsts, sems = rest[26:]
    copies = [
        pltpu.make_async_copy(
            rest[4 * part + n].at[pl.ds(0, 4 * BLOCK)],
            kv_all.at[n, pl.ds(4 * part * BLOCK, 4 * BLOCK)],
            sems.at[4 * part + n],
        )
        for part in range(4)
        for n in range(4)
    ]
    early = (8, 9, 12, 13)
    for n in early:
        copies[n].start()
    for n in range(16):
        if n not in early:
            copies[n].start()
    fill_starts(starts, firsts, table, bounds)
    top[...] = top_near[...]
    total[...] = total_near[...]
    gq_all[...] = jnp.zeros(gq_all.shape, jnp.float32)
    grad_all[...] = jnp.zeros(grad_all.shape, jnp.bfloat16)
    for n in early:
        copies[n].wait()

    add_to_sums(table, firsts, small, range(8, 16), kv_all, bias, starts, top, total, q_turned)
    for row in range(2 * GROUP):
        best = jnp.max(top[row], axis=0, keepdims=True)
        amount = jnp.sum(total[row] * jnp.exp2(top[row] - best), axis=0, keepdims=True)
        lse[pl.ds(row, 1), :] = best + jnp.log2(amount)
    for n in range(16):
        if n not in early:
            copies[n].wait()

    def add_gradients(t, carry):
        j, which = t // 2, t % 2
        rel, dc = j // 2, j % 2

        @pl.when(needed(table, firsts, which, j))
        def _():
            again = (which == 1) & needed(table, firsts, 0, j)
            fill_bias(bias, starts, table, which, table[0, j])
            k = kv_all[dc, block_at(table[4 + dc, rel]), :]
            v = kv_all[2 + dc, block_at(table[6 + dc, rel]), :]

            @pl.when(jnp.logical_not(again))
            def _():
                key_turned[...] = k.T
                held_sums[...] = jnp.zeros(held_sums.shape, jnp.float32)

            turned = key_turned[...]

            def first(h):
                row = which * GROUP + h
                return dot(k, q_turned[row], (1, 0)), dot(v, d_turned[row], (1, 0))

            def middle(h, s, dp):
                row = which * GROUP + h
                p = jnp.exp2(s * FACTOR + bias[...] - lse[pl.ds(row, 1), :])
                ds = (p * (dp - delta[pl.ds(row, 1), :])).astype(jnp.bfloat16)
                return p.astype(jnp.bfloat16), ds

            early, late = {}, {}
            gk_sum, gv_sum = held_sums[0], held_sums[1]
            for step in range(GROUP + 2):
                if step < GROUP:
                    early[step] = first(step)
                h = step - 1
                if 0 <= h < GROUP:
                    late[h] = middle(h, *early.pop(h))
                h = step - 2
                if 0 <= h < GROUP:
                    row = which * GROUP + h
                    p, ds = late.pop(h)
                    gv_sum = gv_sum + dot(d_turned[row], p, (1, 1))
                    gk_sum = gk_sum + dot(q_turned[row], ds, (1, 1))
                    gq_all[row] += dot(turned, ds, (1, 0))
            held_sums[0], held_sums[1] = gk_sum, gv_sum
            grad_all[dc, table[8 + dc, rel]] = (gk_sum * SCALE).T.astype(jnp.bfloat16)
            grad_all[2 + dc, table[10 + dc, rel]] = gv_sum.T.astype(jnp.bfloat16)

        return carry

    lax.fori_loop(0, 64, add_gradients, 0)
    outs = []
    for n in range(4):
        outs.append(pltpu.make_async_copy(grad_all.at[n, pl.ds(8, 8)], send[n], sems.at[2 * n + 1]))
        outs.append(pltpu.make_async_copy(grad_all.at[n, pl.ds(0, 8)], keep[n], sems.at[2 * n]))
    for copy in outs:
        copy.start()
    for which in (1, 0):
        for h in range(GROUP):
            turned = (gq_all[which * GROUP + h] * SCALE).T.astype(jnp.bfloat16)
            gq_out[which, :, pl.ds(h * HD, HD)] = turned
        outs.append(pltpu.make_async_copy(gq_out.at[which], gq[which], sems.at[8 + which]))
        outs[-1].start()
    for copy in outs:
        copy.wait()


SMEM = pl.BlockSpec(memory_space=pltpu.SMEM)
VMEM = pl.BlockSpec(memory_space=pltpu.VMEM)
ANY = pl.BlockSpec(memory_space=pl.ANY)
HBM = pl.BlockSpec(memory_space=pltpu.HBM)
TURNED = jax.ShapeDtypeStruct((2 * GROUP, HD, BLOCK), jnp.bfloat16)


def in_hbm(*arrays):
    return [pltpu.with_memory_space_constraint(array, pltpu.HBM) for array in arrays]


def pack_keys(placement, doc_ids, keys, values):
    half = jax.ShapeDtypeStruct((BLOCK, HD), jnp.bfloat16)
    return pl.pallas_call(
        pack_keys_kernel,
        out_shape=[half] * 4 + [jax.ShapeDtypeStruct((1, HD), jnp.int32)],
        in_specs=[SMEM, VMEM, ANY, ANY],
        out_specs=[VMEM] * 5,
        scratch_shapes=[pltpu.SemaphoreType.DMA((4,))],
        cost_estimate=pl.CostEstimate(flops=1000, bytes_accessed=1 << 19, transcendentals=0),
        name="pack_keys",
    )(placement, doc_ids, keys, values)


def pack_queries(query, d_out, saved):
    return pl.pallas_call(
        pack_queries_kernel,
        out_shape=jax.ShapeDtypeStruct((3, BLOCK, WIDE), jnp.bfloat16),
        in_specs=[ANY] * 3,
        out_specs=VMEM,
        scratch_shapes=[pltpu.SemaphoreType.DMA((3,))],
        cost_estimate=pl.CostEstimate(flops=1000, bytes_accessed=3 << 20, transcendentals=0),
        name="pack_queries",
    )(*in_hbm(query, d_out, saved))


def prepare(query, d_out, saved, swapped, after):
    return pl.pallas_call(
        prepare_kernel,
        out_shape=[
            TURNED,
            TURNED,
            jax.ShapeDtypeStruct((2 * GROUP, BLOCK), jnp.float32),
            jax.ShapeDtypeStruct((1,), jnp.int32),
        ],
        in_specs=[ANY] * 3 + [VMEM, ANY],
        out_specs=[VMEM] * 3 + [SMEM],
        scratch_shapes=[pltpu.VMEM((3, BLOCK, WIDE), jnp.bfloat16), pltpu.SemaphoreType.DMA((3,))],
        compiler_params=pltpu.CompilerParams(vmem_limit_bytes=16 * 1024 * 1024),
        cost_estimate=pl.CostEstimate(flops=2_000_000, bytes_accessed=5 << 20, transcendentals=0),
        name="prepare",
    )(*in_hbm(query, d_out, saved), swapped, after)


def near_sums(table, bounds, small, q_turned, held, come):
    state = jax.ShapeDtypeStruct((2 * GROUP, 8, BLOCK), jnp.float32)
    return pl.pallas_call(
        near_sums_kernel,
        out_shape=[state, state],
        in_specs=[SMEM] * 3 + [VMEM] + [ANY] * 4,
        out_specs=[VMEM] * 2,
        scratch_shapes=[
            pltpu.VMEM((2, 8 * BLOCK, HD), jnp.bfloat16),
            pltpu.VMEM((BLOCK, BLOCK), jnp.float32),
            pltpu.VMEM((8, BLOCK), jnp.int32),
            pltpu.SMEM((2,), jnp.int32),
            pltpu.SemaphoreType.DMA((4,)),
        ],
        compiler_params=pltpu.CompilerParams(vmem_limit_bytes=12 * 1024 * 1024),
        cost_estimate=pl.CostEstimate(flops=1_000_000_000, bytes_accessed=2 << 20, transcendentals=8 << 20),
        name="near_sums",
    )(table, bounds, small, q_turned, *held[:2], *come[:2])


def gradients(table, bounds, small, turned, sums, blocks):
    part = jax.ShapeDtypeStruct((8, BLOCK, HD), jnp.bfloat16)
    return pl.pallas_call(
        main_kernel,
        out_shape=[pltpu.HBM((BLOCK, WIDE), jnp.bfloat16)] * 2
        + [part] * 4
        + [pltpu.HBM((8, BLOCK, HD), jnp.bfloat16)] * 4,
        in_specs=[SMEM] * 3 + [VMEM] * 5 + [ANY] * 16,
        out_specs=[HBM] * 2 + [ANY] * 4 + [HBM] * 4,
        scratch_shapes=[
            pltpu.VMEM((4, 16 * BLOCK, HD), jnp.bfloat16),
            pltpu.VMEM((4, 16, BLOCK, HD), jnp.bfloat16),
            pltpu.VMEM((2 * GROUP, HD, BLOCK), jnp.float32),
            pltpu.VMEM((2 * GROUP, 8, BLOCK), jnp.float32),
            pltpu.VMEM((2 * GROUP, 8, BLOCK), jnp.float32),
            pltpu.VMEM((2 * GROUP, BLOCK), jnp.float32),
            pltpu.VMEM((2, BLOCK, WIDE), jnp.bfloat16),
            pltpu.VMEM((2, HD, BLOCK), jnp.float32),
            pltpu.VMEM((BLOCK, BLOCK), jnp.float32),
            pltpu.VMEM((HD, BLOCK), jnp.bfloat16),
            pltpu.VMEM((8, BLOCK), jnp.int32),
            pltpu.SMEM((2,), jnp.int32),
            pltpu.SemaphoreType.DMA((16,)),
        ],
        compiler_params=pltpu.CompilerParams(vmem_limit_bytes=20 * 1024 * 1024),
        cost_estimate=pl.CostEstimate(flops=12_000_000_000, bytes_accessed=10 << 20, transcendentals=16 << 20),
        name="gradients",
    )(table, bounds, small, *turned, *sums, *blocks)


def gather(parts, edges):
    held = [part[None] for part in parts]
    for step in range(3):
        sent = list(held)
        if step > 0:
            rows = jnp.broadcast_to(pack_edges(edges)[None], (held[0].shape[0], STAT_ROWS, HD))
            sent[0] = jnp.concatenate([held[0], rows], axis=1)
        come = [across(sent[n], (n + step) % 4) for n in range(4)]
        if step == 0:
            edges = jnp.maximum(edges, across(edges, 0))
        else:
            edges = jnp.maximum(edges, unpack_edges(come[0]))
            come[0] = come[0][:, :BLOCK]
        if step < 2:
            held = [jnp.concatenate(pair, axis=0) for pair in zip(held, come)]
            held = lax.optimization_barrier(held)
    far_held = [across(held[n], (n + 3) % 4) for n in range(4)]
    far_come = [across(come[n], (n + 3) % 4) for n in range(4)]
    edges = jnp.maximum(edges, across(edges, 3))
    return [array.reshape(4 * BLOCK, HD) for array in held + come + far_held + far_come], edges


def pack_edges(edges):
    spare = jnp.zeros((STAT_ROWS - 2, HD), jnp.int32)
    return jnp.concatenate([edges // 128, edges % 128, spare], axis=0).astype(jnp.bfloat16)


def unpack_edges(array):
    rows = array[:1, BLOCK : BLOCK + 2].astype(jnp.float32)
    return (rows[:, 0] * 128 + rows[:, 1]).astype(jnp.int32)


def reduce(keep, send, gq_mine, gq_other, side_by_side):
    for step in range(4):
        if step == 3:
            moved = swap(jnp.stack([keep[1], keep[3]]))
            keep = [keep[0], moved[0], keep[2], moved[1]]
        come = [across(array, (n + step) % 4, n % 2 if step == 3 else 0) for n, array in enumerate(send)]
        total = [
            (a.astype(jnp.float32) + b.astype(jnp.float32)).astype(jnp.bfloat16) for a, b in zip(keep, come)
        ]
        if step == 3:
            return [a[0] for a in total], gq
        if step == 1:
            total[3], gq_other = lax.optimization_barrier((total[3], gq_other))
            gq = side_by_side(gq_mine, swap(gq_other))
        if step == 2:
            total[3], gq = lax.optimization_barrier((total[3], gq))
        half = total[0].shape[0] // 2
        keep, send = [a[:half] for a in total], [a[half:] for a in total]


def shards(query, keys, values, out_saved, d_out, doc_ids, placement, block_keys):
    me = lax.axis_index("ctx")
    core = me % 2
    z, y = me // 8, (me // 2) % 4

    k_mine, v_mine, k_other, v_other, edges = pack_keys(placement, doc_ids[None], keys, values)
    k_swap, v_swap = swap(k_other), swap(v_other)
    query, d_out, out_saved, _ = lax.optimization_barrier((query, d_out, out_saved, k_other))
    swapped = swap(pack_queries(query, d_out, out_saved))
    edges, k_swap = lax.optimization_barrier((edges, k_swap))
    for_x = [lax.ppermute(edges, "head", [(i, (i + r) % 4) for i in range(4)]) for r in (1, 2, 3)]
    edges = jnp.maximum(jnp.maximum(edges, for_x[0]), jnp.maximum(for_x[1], for_x[2]))
    edges = jnp.maximum(edges, swap(edges))
    blocks, bounds = gather([k_mine, k_swap, v_mine, v_swap], edges)
    *turned, small = prepare(query, d_out, out_saved, swapped, blocks[1])

    j = jnp.arange(32)
    slots = index_of((gray(z) * 4 + gray(y)) ^ (j // 2), core ^ (j % 2))
    block_of = jnp.sum(jnp.where(slots[:, None] == jnp.arange(32)[None, :], placement[None, :], 0), axis=1)
    own = block_of[:2]
    chosen = jnp.sum(jnp.where(own[:, None, None] == jnp.arange(32)[None, :, None], block_keys[None], 0), axis=1)
    listed = jnp.any(chosen[:, :, None] == block_of[None, None, :], axis=1).astype(jnp.int32)
    bits = [[(rel >> bit) & 1 for bit in range(4)] for rel in range(32)]
    gathered = [[sum(b[(n + k) % 4] << k for k in range(4)) for b in bits] for n in range(4)]
    reduced = [[sum(b[(n + k) % 4] << (3 - k) for k in range(4)) for b in bits] for n in range(4)]
    order = [[gathered[n].index(place % 16) for place in range(32)] for n in range(2)]
    table = jnp.concatenate(
        [block_of[None], listed, block_of[None], jnp.array(gathered), jnp.array(reduced), jnp.array(order)], axis=0
    ).astype(jnp.int32)

    sums = near_sums(table, bounds, small, turned[0], blocks[0:4], blocks[4:8])
    outs = gradients(table, bounds, small, turned, sums, blocks)
    def side_by_side(mine, other):
        return jnp.where(
            core == 0, jnp.concatenate([mine, other], axis=1), jnp.concatenate([other, mine], axis=1)
        )

    (gk_mine, gk_other, gv_mine, gv_other), gq = reduce(outs[2:6], outs[6:10], *outs[:2], side_by_side)
    return gq, side_by_side(gk_mine, gk_other), side_by_side(gv_mine, gv_other)


def solution(mesh):
    placed = (
        P("ctx", "head"),
        P("ctx", "head"),
        P("ctx", "head"),
        P("ctx", "head"),
        P("ctx", "head"),
        P(("ctx", "head")),
        P(),
        P(),
    )
    return jax.shard_map(
        shards,
        mesh=mesh,
        in_specs=placed,
        out_specs=(P("ctx", "head"), P("ctx", "head"), P("ctx", "head")),
        check_vma=False,
    )
```
